128 devices in a mesh: dp: 8 (over z_hi, x), tensor: 16 (over z_lo, y, core).
Axes of the slice: x: 4, y: 4, z: 4 (z_hi: 2, z_lo: 2; z = z_hi * 2 + z_lo), core: 2. Of those that a mesh axis runs over, the one named last changes fastest.
Arguments:
- tokens: bfloat16 [16384, 2048], P(('dp', 'tensor')), may hold values from -6 to 6
- gain: float32 [2048], replicated, may hold values from 0.25 to 1.75
- gate_saved: bfloat16 [16384, 8192], P('dp', 'tensor'), may hold values from -12 to 12
- up_saved: bfloat16 [16384, 8192], P('dp', 'tensor'), may hold values from -6 to 6
- out_grad: bfloat16 [16384, 2048], P(('dp', 'tensor')), may hold values from -6 to 6
- gate_weight: bfloat16 [2048, 8192], P(None, 'tensor'), may hold values from -0.125 to 0.125
- up_weight: bfloat16 [2048, 8192], P(None, 'tensor'), may hold values from -0.125 to 0.125
- down_weight: bfloat16 [8192, 2048], P('tensor'), may hold values from -0.0625 to 0.0625
Outputs:
- token_grad: bfloat16 [16384, 2048], P(('dp', 'tensor'))
- gain_grad: float32 [2048], replicated
- gate_grad: bfloat16 [2048, 8192], P('dp', 'tensor')
- up_grad: bfloat16 [2048, 8192], P('dp', 'tensor')
- down_grad: bfloat16 [8192, 2048], P('tensor', 'dp')
The draws below stay inside these ranges and needn't reach their ends.
All inputs are finite; a program needn't handle non-finite values.
Results may differ from the reference program's by a relative error of at most 0.022.
Values may be sent and summed in bfloat16 or wider, within the bound.
No kernel may reach another device: no remote copies, remote signals or barrier semaphores. Data moves between devices by JAX's collectives and lax.ppermute only.
A program may use at most 128 MiB of HBM per device.

```python
import jax
import jax.numpy as jnp
from jax import lax

D = 2048
FF = 8192
TOKENS = 16384
N_DP = 8
N_TENSOR = 16


def block_scale(stream_key, dims, cuts, least, high):
    def one(dim, shards_of):
        heights = jax.random.uniform(jax.random.fold_in(jax.random.fold_in(stream_key, 6), dim), (shards_of,), jnp.float32, least / len(cuts), high / len(cuts))
        return jnp.repeat(jnp.exp(heights), dims[dim] // shards_of).reshape((-1,) + (1,) * (len(dims) - dim - 1))

    level = one(*cuts[0])
    for cut in cuts[1:]:
        level = level * one(*cut)
    return level


def bell_draw(stream_key, extent, scale, reach, split=(), held_as=jnp.bfloat16):
    result = jax.random.normal(stream_key, extent, jnp.float32) * scale
    if len(split) > 0:
        result = block_scale(stream_key, extent, split, -0.22, 0.18) * result
    return jnp.clip(result, min=-reach, max=reach).astype(held_as)


def setup_inputs(seed: int = 0) -> dict:
    streams_of = jax.random.split(jax.random.key(seed), 9)
    tokens = bell_draw(streams_of[0], (TOKENS, D), 1.0, 6.0, ((0, 128),))
    gain = jnp.clip(1.0 + 0.15 * jax.random.normal(streams_of[1], (D,), jnp.float32), 0.25, 1.75)
    gate_saved = bell_draw(streams_of[2], (TOKENS, FF), 2.0, 12.0, ((0, 8), (1, 16)))
    up_saved = bell_draw(streams_of[3], (TOKENS, FF), 1.0, 6.0, ((0, 8), (1, 16)))
    out_grad = bell_draw(streams_of[4], (TOKENS, D), 1.0, 6.0, ((0, 128),))
    gate_weight = bell_draw(streams_of[5], (D, FF), D ** -0.5, 0.125, ((1, 16),))
    up_weight = bell_draw(streams_of[6], (D, FF), D ** -0.5, 0.125, ((1, 16),))
    down_weight = bell_draw(streams_of[7], (FF, D), FF ** -0.5, 0.0625, ((0, 16),))
    return {"tokens": tokens, "gain": gain, "gate_saved": gate_saved, "up_saved": up_saved, "out_grad": out_grad, "gate_weight": gate_weight, "up_weight": up_weight, "down_weight": down_weight}


def group_terms(normed_g, act_g, dy_g, gate_g, up_g, gate_weight, up_weight, down_weight):
    hidden_grad = lax.dot_general(dy_g, down_weight, (((1,), (1,)), ((), ())), preferred_element_type=jnp.float32)
    gate_f = gate_g.astype(jnp.float32)
    sigma = jax.nn.sigmoid(gate_f)
    gate_delta = (hidden_grad * up_g.astype(jnp.float32) * sigma * (1.0 + gate_f * (1.0 - sigma))).astype(jnp.bfloat16)
    up_delta = (hidden_grad * gate_f * sigma).astype(jnp.bfloat16)
    down_part = lax.dot_general(act_g, dy_g, (((0,), (0,)), ((), ())), preferred_element_type=jnp.float32).astype(jnp.bfloat16)
    gate_part = lax.dot_general(normed_g, gate_delta, (((0,), (0,)), ((), ())), preferred_element_type=jnp.float32).astype(jnp.bfloat16)
    up_part = lax.dot_general(normed_g, up_delta, (((0,), (0,)), ((), ())), preferred_element_type=jnp.float32).astype(jnp.bfloat16)
    block = FF // N_TENSOR
    rows = gate_delta.shape[0]
    gd = gate_delta.reshape(rows, N_TENSOR, block).transpose(1, 0, 2)
    ud = up_delta.reshape(rows, N_TENSOR, block).transpose(1, 0, 2)
    gw = gate_weight.reshape(D, N_TENSOR, block).transpose(1, 0, 2)
    uw = up_weight.reshape(D, N_TENSOR, block).transpose(1, 0, 2)

    def add_block(total, pieces):
        a, b, c, e = pieces
        term = lax.dot_general(a, c, (((1,), (1,)), ((), ())), preferred_element_type=jnp.float32)
        term = term + lax.dot_general(b, e, (((1,), (1,)), ((), ())), preferred_element_type=jnp.float32)
        return (total + term.astype(jnp.bfloat16).astype(jnp.float32), None)
    normed_grad, _ = lax.scan(add_block, jnp.zeros((rows, D), jnp.float32), (gd, ud, gw, uw))
    return (down_part, gate_part, up_part, normed_grad)

def reference(tokens, gain, gate_saved, up_saved, out_grad, gate_weight, up_weight, down_weight):
    x = tokens.astype(jnp.float32)
    inverse = lax.rsqrt(lax.optimization_barrier(jnp.mean(x * x, axis=-1, keepdims=True)) + 1e-05)
    normed = (x * inverse * gain).astype(jnp.bfloat16)
    gate_f = gate_saved.astype(jnp.float32)
    activated = (gate_f * jax.nn.sigmoid(gate_f) * up_saved.astype(jnp.float32)).astype(jnp.bfloat16)
    rows = TOKENS // N_DP

    def one_group(pieces):
        return group_terms(*pieces, gate_weight, up_weight, down_weight)
    down_parts, gate_parts, up_parts, normed_grad = lax.map(one_group, (normed.reshape(N_DP, rows, D), activated.reshape(N_DP, rows, FF), out_grad.reshape(N_DP, rows, D), gate_saved.reshape(N_DP, rows, FF), up_saved.reshape(N_DP, rows, FF)))
    down_grad = lax.optimization_barrier(jnp.sum(down_parts.astype(jnp.float32), axis=0)).astype(jnp.bfloat16)
    gate_grad = lax.optimization_barrier(jnp.sum(gate_parts.astype(jnp.float32), axis=0)).astype(jnp.bfloat16)
    up_grad = lax.optimization_barrier(jnp.sum(up_parts.astype(jnp.float32), axis=0)).astype(jnp.bfloat16)
    normed_grad = normed_grad.reshape(TOKENS, D)
    unit = x * inverse
    gain_grad = lax.optimization_barrier(jnp.sum(normed_grad * unit, axis=0))
    scaled = gain * normed_grad
    mean_term = lax.optimization_barrier(jnp.mean(scaled * unit, axis=-1, keepdims=True))
    token_grad = (out_grad.astype(jnp.float32) + inverse * (scaled - unit * mean_term)).astype(jnp.bfloat16)
    return (token_grad, gain_grad, gate_grad, up_grad, down_grad)
```

```python
import functools

import jax
import jax.numpy as jnp
import numpy as np
from jax import lax
from jax.experimental import pallas as pl
from jax.experimental.pallas import tpu as pltpu
from jax.sharding import Mesh, PartitionSpec as P

AXES = ("zh", "x", "zl", "y", "c")
SIZES = (2, 4, 2, 4, 2)
D = 2048
ROWS = 128
F = 512
BF = jnp.bfloat16
F32 = jnp.float32
MIB = 1024 * 1024


def send(value, **shift):
    ids = np.arange(128).reshape(SIZES)
    pairs = []
    for at in np.ndindex(*SIZES):
        to = tuple((a + shift.get(n, 0)) % s for a, n, s in zip(at, AXES, SIZES))
        pairs.append((int(ids[at]), int(ids[to])))
    return lax.ppermute(value, AXES, pairs)


def nt(a, b):
    return lax.dot_general(a, b, (((1,), (1,)), ((), ())), preferred_element_type=F32)


def nn(a, b):
    return lax.dot_general(a, b, (((1,), (0,)), ((), ())), preferred_element_type=F32)


def rows_of(ref, s_ref):
    return jnp.concatenate([ref[s_ref[p]] for p in range(8)], axis=0).astype(F32)


def down_kernel(s_ref, go, uo, gx, ux, *rest):
    dy, (out_own, out_oth, act_t) = rest[:8], rest[8:]

    @pl.when(pl.program_id(0) == 0)
    def _():
        for k, (g_ref, u_ref) in enumerate(((go.at[:, 0], uo.at[:, 0]), (gx.at[0], ux.at[0]))):
            for p in range(8):
                g = g_ref[s_ref[p]].astype(F32)
                u = u_ref[s_ref[p]].astype(F32)
                act = g * u / (1.0 + jnp.exp(-g))
                act_t[k * F : (k + 1) * F, p * ROWS : (p + 1) * ROWS] = act.T.astype(BF)

    cols = jnp.concatenate([d[...] for d in dy], axis=0)
    out_own[0] = nn(act_t[:F], cols).astype(BF)
    out_oth[0] = nn(act_t[F:], cols).astype(BF)


def down_call(scalars, gate4, up4, swapped, dy):
    grid_spec = pltpu.PrefetchScalarGridSpec(
        num_scalar_prefetch=1,
        grid=(8,),
        in_specs=[pl.BlockSpec((8, 1, ROWS, F), lambda i, s: (0, s[8], 0, 0))] * 2
        + [
            pl.BlockSpec((1, 8, ROWS, F), lambda i, s: (0, 0, 0, 0)),
            pl.BlockSpec((1, 8, ROWS, F), lambda i, s: (1, 0, 0, 0)),
        ]
        + [pl.BlockSpec((ROWS, 256), lambda i, s: (0, s[9 + i]))] * 8,
        out_specs=[pl.BlockSpec((1, F, 256), lambda i, s: (i, 0, 0))] * 2,
        scratch_shapes=[pltpu.VMEM((2 * F, 8 * ROWS), BF)],
    )
    return pl.pallas_call(
        down_kernel,
        grid_spec=grid_spec,
        out_shape=[jax.ShapeDtypeStruct((8, F, 256), BF)] * 2,
        compiler_params=pltpu.CompilerParams(vmem_limit_bytes=40 * MIB),
        cost_estimate=pl.CostEstimate(
            flops=2 * 1024 * 1024 * D, bytes_accessed=12 * MIB, transcendentals=1024 * 1024
        ),
        name="down",
    )(scalars, gate4, up4, swapped, swapped, *dy)


def delta_kernel(s_ref, go, uo, gx, ux, wdo, wgo, wuo, wdx, wgx, wux, *rest):
    dy = rest[:8]
    gd, ud, n_own, n_z, n_yp, n_ym, n_2, n_z2, rows, acc, sem = rest[8:]
    h = pl.program_id(0)

    @pl.when(h == 0)
    def _():
        copies = [
            pltpu.make_async_copy(d, rows.at[pl.ds(p * ROWS, ROWS)], sem.at[p])
            for p, d in enumerate(dy)
        ]
        for copy in copies:
            copy.start()
        for copy in copies:
            copy.wait()

    def part(g_ref, u_ref, wd, wg, wu):
        hidden = nt(rows[...], wd[...])
        g = rows_of(g_ref, s_ref)
        u = rows_of(u_ref, s_ref)
        sigma = 1.0 / (1.0 + jnp.exp(-g))
        hs = hidden * sigma
        gate_delta = (hs * u * (1.0 + g * (1.0 - sigma))).astype(BF)
        up_delta = (hs * g).astype(BF)
        gd[...] = gate_delta
        ud[...] = up_delta
        for n in range(4):
            at = slice(n * 512, (n + 1) * 512)
            term = nt(gate_delta, wg[at, :]) + nt(up_delta, wu[at, :])

            @pl.when(h == 0)
            def _():
                acc[:, at] = term

            @pl.when(h > 0)
            def _():
                acc[:, at] += term

    @pl.when(h < 2)
    def _():
        part(go.at[:, 0], uo.at[:, 0], wdo, wgo, wuo)

    @pl.when(h >= 2)
    def _():
        part(gx.at[0], ux.at[0], wdx, wgx, wux)

    @pl.when(h == 3)
    def _():
        for p, out in enumerate(
            (n_own, n_z, n_ym.at[0], n_yp.at[0], n_2, n_ym.at[1], n_yp.at[1], n_z2)
        ):
            out[...] = acc[p * ROWS : (p + 1) * ROWS].astype(BF)


def delta_call(scalars, gate4, up4, swapped, own, other, dy):
    def low(i):
        return jnp.minimum(i, 1)

    def high(i):
        return jnp.maximum(i - 2, 0)

    piece = jax.ShapeDtypeStruct((ROWS, D), BF)
    pair = jax.ShapeDtypeStruct((2, ROWS, D), BF)
    wide = jax.ShapeDtypeStruct((8 * ROWS, 2 * F), BF)
    whole = pl.BlockSpec((ROWS, D), lambda i, s: (0, 0))
    whole2 = pl.BlockSpec((2, ROWS, D), lambda i, s: (0, 0, 0))
    grid_spec = pltpu.PrefetchScalarGridSpec(
        num_scalar_prefetch=1,
        grid=(4,),
        in_specs=[pl.BlockSpec((8, 1, ROWS, 256), lambda i, s: (0, s[8], 0, low(i)))] * 2
        + [
            pl.BlockSpec((1, 8, ROWS, 256), lambda i, s: (0, 0, 0, high(i))),
            pl.BlockSpec((1, 8, ROWS, 256), lambda i, s: (1, 0, 0, high(i))),
            pl.BlockSpec((256, D), lambda i, s: (low(i), 0)),
            pl.BlockSpec((D, 256), lambda i, s: (0, low(i))),
            pl.BlockSpec((D, 256), lambda i, s: (0, low(i))),
            pl.BlockSpec((256, D), lambda i, s: (high(i), 0)),
            pl.BlockSpec((D, 256), lambda i, s: (0, high(i))),
            pl.BlockSpec((D, 256), lambda i, s: (0, high(i))),
        ]
        + [pl.BlockSpec(memory_space=pl.ANY)] * 8,
        out_specs=[pl.BlockSpec((8 * ROWS, 256), lambda i, s: (0, i))] * 2
        + [whole, whole, whole2, whole2, whole, whole],
        scratch_shapes=[
            pltpu.VMEM((8 * ROWS, D), BF),
            pltpu.VMEM((8 * ROWS, D), F32),
            pltpu.SemaphoreType.DMA((8,)),
        ],
    )
    return pl.pallas_call(
        delta_kernel,
        grid_spec=grid_spec,
        out_shape=[wide, wide, piece, piece, pair, pair, piece, piece],
        compiler_params=pltpu.CompilerParams(vmem_limit_bytes=56 * MIB),
        cost_estimate=pl.CostEstimate(
            flops=6 * 1024 * 1024 * D, bytes_accessed=32 * MIB, transcendentals=1024 * 1024
        ),
        name="deltas",
    )(scalars, gate4, up4, swapped, swapped, *own, *other, *dy)


def weight_kernel(s_ref, gd, ud, gain, wgo, wuo, wgx, wux, *rest):
    unit, (out_own, out_oth, out_gain) = rest[:8], rest[8:]
    lhs = jnp.concatenate([u[...] for u in unit], axis=1)
    scale = gain[...]
    total = jnp.zeros((256, 128), F32)
    for delta, at, w_own, w_oth in ((gd, 0, wgo, wgx), (ud, F, wuo, wux)):
        for half, w, out in ((0, w_own, out_own), (F, w_oth, out_oth)):
            grad = nn(lhs, delta[:, half : half + F])
            out[0, :, at : at + F] = (grad * scale).astype(BF)
            prod = grad * w[...].astype(F32)
            for k in range(4):
                total = total + prod[:, k * 128 : (k + 1) * 128]
    out_gain[0] = total


def weight_call(scalars, gd, ud, gain, own, other, unit):
    full = pl.BlockSpec((8 * ROWS, 2 * F), lambda i, s: (0, 0))
    rows = pl.BlockSpec((256, F), lambda i, s: (s[9 + i], 0))
    grid_spec = pltpu.PrefetchScalarGridSpec(
        num_scalar_prefetch=1,
        grid=(8,),
        in_specs=[full, full, pl.BlockSpec((256, 1), lambda i, s: (s[9 + i], 0))]
        + [rows] * 4
        + [pl.BlockSpec((256, ROWS), lambda i, s: (s[9 + i], 0))] * 8,
        out_specs=[
            pl.BlockSpec((1, 256, 2 * F), lambda i, s: (i, 0, 0)),
            pl.BlockSpec((1, 256, 2 * F), lambda i, s: (i, 0, 0)),
            pl.BlockSpec((1, 256, 128), lambda i, s: (s[9 + i], 0, 0)),
        ],
    )
    return pl.pallas_call(
        weight_kernel,
        grid_spec=grid_spec,
        out_shape=[jax.ShapeDtypeStruct((8, 256, 2 * F), BF)] * 2
        + [jax.ShapeDtypeStruct((8, 256, 128), F32)],
        compiler_params=pltpu.CompilerParams(vmem_limit_bytes=40 * MIB),
        cost_estimate=pl.CostEstimate(
            flops=4 * 1024 * 1024 * D, bytes_accessed=24 * MIB, transcendentals=0
        ),
        name="weights",
    )(scalars, gd, ud, gain, *own, *other, *unit)


def gather(own):
    from_z = send(own, zl=1)
    from_2 = send(own, y=2)
    from_m = send(own, y=1)
    from_p = send(own, y=-1)
    from_zm = send(from_z, y=1)
    from_zp = send(from_z, y=-1)
    from_z2 = send(from_2, zl=1)
    return (own, from_z, from_m, from_p, from_2, from_zm, from_zp, from_z2)


def total_of(*terms):
    out = terms[0].astype(F32)
    for term in terms[1:]:
        out = out + term.astype(F32)
    return out


def over_dp(own, other):
    back = send(other, c=1)
    parts = [
        total_of(own[2 * r : 2 * r + 2], back[2 * r : 2 * r + 2]) for r in range(4)
    ]
    got = [send(parts[r].astype(BF), x=r) for r in (1, 2, 3)]
    both = total_of(parts[0], *got)
    return both[0] + send(both[1].astype(BF), zh=1).astype(F32)


def local(tokens, gain, gate_saved, up_saved, out_grad, gate_weight, up_weight, down_weight):
    zh, x_at, zl, y, c = (lax.axis_index(a) for a in AXES)
    oz = 1 - zl
    places = [zl * 4 + y, oz * 4 + y]
    places += [zl * 4 + (y + k) % 4 for k in (3, 1, 2)]
    places += [oz * 4 + (y + k) % 4 for k in (3, 1, 2)]
    order = [((zh + q) % 2) * 4 + (x_at + r) % 4 for r in range(4) for q in range(2)]
    scalars = jnp.stack(places + [c] + order).astype(jnp.int32)

    dy = gather(out_grad)

    gate4 = gate_saved.reshape(8, 2, ROWS, F)
    up4 = up_saved.reshape(8, 2, ROWS, F)
    theirs = jnp.stack(
        [lax.dynamic_index_in_dim(a, 1 - c, 1, keepdims=False) for a in (gate4, up4)]
    )
    swapped = send(theirs, c=1)
    down_other = send(down_weight, c=1)
    gate_other = send(gate_weight, c=1)
    up_other = send(up_weight, c=1)

    x = tokens.astype(F32)
    inverse = lax.rsqrt(jnp.mean(x * x, axis=-1, keepdims=True) + 1e-05)
    unit = x * inverse
    units = gather(unit.astype(BF).T)

    down_own, down_oth = down_call(scalars, gate4, up4, swapped, dy)
    down_sum = over_dp(down_own, down_oth)

    gd, ud, n_own, n_z, n_yp, n_ym, n_2, n_z2 = delta_call(
        scalars,
        gate4,
        up4,
        swapped,
        (down_weight, gate_weight, up_weight),
        (down_other, gate_other, up_other),
        dy,
    )
    a = send(n_yp, y=1)
    b = send(n_ym, y=-1)
    d = send(n_z2, zl=1)

    w_own, w_oth, gain_part = weight_call(
        scalars,
        gd,
        ud,
        gain.reshape(D, 1),
        (gate_weight, up_weight),
        (gate_other, up_other),
        units,
    )
    gain_grad = lax.psum(jnp.sum(gain_part, axis=-1).reshape(D), AXES)
    both_sum = over_dp(w_own, w_oth)

    e = send(total_of(n_2, d).astype(BF), y=2)
    f = send(total_of(n_z, a[1], b[1]).astype(BF), zl=1)
    normed_grad = total_of(n_own, a[0], b[0], e, f)
    scaled = gain * normed_grad
    mean_term = jnp.mean(scaled * unit, axis=-1, keepdims=True)
    token_grad = (out_grad.astype(F32) + inverse * (scaled - unit * mean_term)).astype(BF)
    return (
        token_grad,
        gain_grad,
        both_sum[:, :F].astype(BF),
        both_sum[:, F:].astype(BF),
        down_sum.astype(BF),
    )


def solution(mesh):
    mesh = Mesh(mesh.devices.reshape(SIZES), AXES)
    dp, tensor = ("zh", "x"), ("zl", "y", "c")
    placed = (
        P(dp + tensor, None),
        P(),
        P(dp, tensor),
        P(dp, tensor),
        P(dp + tensor, None),
        P(None, tensor),
        P(None, tensor),
        P(tensor, None),
    )
    return jax.shard_map(
        local,
        mesh=mesh,
        in_specs=placed,
        out_specs=(
            P(dp + tensor, None),
            P(),
            P(dp, tensor),
            P(dp, tensor),
            P(tensor, dp),
        ),
        check_vma=False,
    )
```

```python
import functools

import jax
import jax.numpy as jnp
import numpy as np
from jax import lax
from jax.experimental import pallas as pl
from jax.experimental.pallas import tpu as pltpu
from jax.sharding import Mesh, PartitionSpec as P

AXES = ("zh", "x", "zl", "y", "c")
SIZES = (2, 4, 2, 4, 2)
D = 2048
ROWS = 128
F = 512
BF = jnp.bfloat16
F32 = jnp.float32
MIB = 1024 * 1024
ANY = pl.BlockSpec(memory_space=pl.ANY)


def send(value, **shift):
    ids = np.arange(128).reshape(SIZES)
    pairs = []
    for at in np.ndindex(*SIZES):
        to = tuple((a + shift.get(n, 0)) % s for a, n, s in zip(at, AXES, SIZES))
        pairs.append((int(ids[at]), int(ids[to])))
    return lax.ppermute(value, AXES, pairs)


def nt(a, b):
    return lax.dot_general(a, b, (((1,), (1,)), ((), ())), preferred_element_type=F32)


def nn(a, b):
    return lax.dot_general(a, b, (((1,), (0,)), ((), ())), preferred_element_type=F32)


def struct(*shape, dtype=BF):
    return jax.ShapeDtypeStruct(shape, dtype)


def params():
    return pltpu.CompilerParams(vmem_limit_bytes=60 * MIB)


def cost(mults=0):
    return pl.CostEstimate(flops=2 * mults + 1024, bytes_accessed=1024, transcendentals=0)


def after(value, *others):
    return lax.optimization_barrier((value, *others))[0]


def first_kernel(s_ref, tokens, gate, up, wg, wu, wd, unit_t, pack):
    @pl.when(pl.program_id(0) == 0)
    def _():
        x = tokens[...].astype(F32)
        unit = x * lax.rsqrt(jnp.mean(x * x, axis=-1, keepdims=True) + 1e-05)
        unit_t[...] = unit.T.astype(BF)

    for j in range(2):
        pack[j, :128] = gate[j, 0]
        pack[j, 128:256] = up[j, 0]
        pack[j, 256:512] = wg[j * 256 : j * 256 + 256]
        pack[j, 512:768] = wu[j * 256 : j * 256 + 256]
        for k in range(4):
            at = 768 + k * 64
            pack[j, at : at + 64] = wd[j * 64 : j * 64 + 64, k * F : k * F + F]


def first_call(scalars, tokens, gate4, up4, wg, wu, wd):
    half = pl.BlockSpec((2, 1, ROWS, F), lambda i, s: (i, 1 - s[8], 0, 0))
    rows = pl.BlockSpec((512, F), lambda i, s: (i, 0))
    return pl.pallas_call(
        first_kernel,
        grid_spec=pltpu.PrefetchScalarGridSpec(
            num_scalar_prefetch=1,
            grid=(4,),
            in_specs=[
                pl.BlockSpec((ROWS, D), lambda i, s: (0, 0)),
                half,
                half,
                rows,
                rows,
                pl.BlockSpec((128, D), lambda i, s: (i, 0)),
            ],
            out_specs=[
                pl.BlockSpec((D, ROWS), lambda i, s: (0, 0)),
                pl.BlockSpec((2, 1024, F), lambda i, s: (i, 0, 0)),
            ],
        ),
        out_shape=[struct(D, ROWS), struct(8, 1024, F)],
        compiler_params=params(),
        cost_estimate=cost(),
        name="first",
    )(scalars, tokens, gate4, up4, wg, wu, wd)


def factor_kernel(s_ref, go, uo, gx, ux, for_gate, for_up, act_t):
    for g, u, at in ((go[0, 0], uo[0, 0], 0), (gx[0], ux[0], F)):
        g = g.astype(F32)
        u = u.astype(F32)
        sigma = 1.0 / (1.0 + jnp.exp(-g))
        silu = g * sigma
        for_up[:, at : at + F] = silu.astype(BF)
        for_gate[:, at : at + F] = (u * sigma * (1.0 + g * (1.0 - sigma))).astype(BF)
        act_t[at : at + F, :] = (silu * u).T.astype(BF)


def factor_call(scalars, gate4, up4, swapped):
    mine = pl.BlockSpec((1, 1, ROWS, F), lambda i, s: (s[i], s[8], 0, 0))
    rows = pl.BlockSpec((ROWS, 2 * F), lambda i, s: (i, 0))
    return pl.pallas_call(
        factor_kernel,
        grid_spec=pltpu.PrefetchScalarGridSpec(
            num_scalar_prefetch=1,
            grid=(8,),
            in_specs=[
                mine,
                mine,
                pl.BlockSpec((1, ROWS, F), lambda i, s: (s[i], 0, 0)),
                pl.BlockSpec((1, ROWS, F), lambda i, s: (s[i], 1, 0)),
            ],
            out_specs=[rows, rows, pl.BlockSpec((2 * F, ROWS), lambda i, s: (0, i))],
        ),
        out_shape=[struct(8 * ROWS, 2 * F)] * 3,
        compiler_params=params(),
        cost_estimate=cost(),
        name="factors",
    )(scalars, gate4, up4, swapped, swapped)


def delta_body(dy, for_gate, for_up, weights, gd, ud, outs, held, sem):
    wd, wg, wu, pack = weights
    wd_own, wd_oth, wg_own, wg_oth, wu_own, wu_oth = held
    moves = ((wd, wd_own), (pack.at[:, 768:1024], wd_oth), (wg, wg_own))
    moves += ((pack.at[:, 256:512], wg_oth), (wu, wu_own), (pack.at[:, 512:768], wu_oth))
    copies = [pltpu.make_async_copy(a, b, sem.at[k]) for k, (a, b) in enumerate(moves)]
    for copy in copies:
        copy.start()
    rows = jnp.concatenate([d[...] for d in dy], axis=0)

    def store(hidden, at):
        gd[:, at] = (hidden * for_gate[:, at].astype(F32)).astype(BF)
        ud[:, at] = (hidden * for_up[:, at].astype(F32)).astype(BF)

    copies[0].wait()
    store(nt(rows, wd_own[...]), slice(0, F))
    copies[1].wait()
    hidden = 0
    for k in range(4):
        block = wd_oth[:, k * 64 : k * 64 + 64, :].reshape(F, F)
        hidden = hidden + nt(rows[:, k * F : k * F + F], block)
    store(hidden, slice(F, 2 * F))
    for copy in copies[2:]:
        copy.wait()
    for n in range(4):
        at, two = slice(n * 512, n * 512 + 512), slice(2 * n, 2 * n + 2)
        out = nt(gd[:, :F], wg_own[at, :])
        out = out + nt(gd[:, F:], wg_oth[two].reshape(F, F))
        out = out + nt(ud[:, :F], wu_own[at, :])
        out = (out + nt(ud[:, F:], wu_oth[two].reshape(F, F))).astype(BF)
        for k, ref in enumerate(outs):
            ref[:, at] = out[k * ROWS : k * ROWS + ROWS]


def delta_kernel_a(*refs):
    dy, (fg, fu), weights, (gd, ud, own, z, ym, yp) = refs[:4], refs[4:6], refs[6:10], refs[-13:-7]
    delta_body(dy, fg, fu, weights, gd, ud, (own, z, ym.at[0], yp.at[0]), refs[-7:-1], refs[-1])


def delta_kernel_b(*refs):
    dy, (fg, fu), weights = refs[:4], refs[4:6], refs[6:10]
    gd, ud, two, ym, yp, z2 = refs[-13:-7]
    delta_body(dy, fg, fu, weights, gd, ud, (two, ym.at[0], yp.at[0], z2), refs[-7:-1], refs[-1])


def delta_call(second, dy, factors, weights, pairs=(), behind=()):
    at = 1 if second else 0
    whole = pl.BlockSpec((ROWS, D), lambda i: (0, 0))
    side = pl.BlockSpec((1, ROWS, D), lambda i: (at, 0, 0))
    wide = pl.BlockSpec((4 * ROWS, 2 * F), lambda i: (at, 0))
    here = pl.BlockSpec((4 * ROWS, 2 * F), lambda i: (0, 0))
    outs = [struct(4 * ROWS, 2 * F)] * 2
    pair = struct(2, ROWS, D)
    if second:
        outs += [struct(ROWS, D), pair, pair, struct(ROWS, D)]
        out_specs = [here, here, whole, side, side, whole]
        aliases = {10: 3, 11: 4}
    else:
        outs += [struct(ROWS, D), struct(ROWS, D), pair, pair]
        out_specs = [here, here, whole, whole, side, side]
        aliases = {}
    extra = (*pairs, *behind)
    return pl.pallas_call(
        delta_kernel_b if second else delta_kernel_a,
        grid=(1,),
        in_specs=[whole] * 4 + [wide] * 2 + [ANY] * 4 + [ANY] * len(extra),
        out_specs=out_specs,
        out_shape=outs,
        scratch_shapes=[pltpu.VMEM((F, D), BF), pltpu.VMEM((8, 256, F), BF)]
        + [pltpu.VMEM((D, F), BF), pltpu.VMEM((8, 256, F), BF)] * 2
        + [pltpu.SemaphoreType.DMA((6,))],
        input_output_aliases=aliases,
        compiler_params=params(),
        cost_estimate=cost(6 * 512 * 1024 * D if second else 0),
        name="deltas_b" if second else "deltas_a",
    )(*dy, *factors, *weights, *extra)


def down_kernel(s_ref, act_t, *refs):
    dy, (out_own, out_oth) = refs[:16], refs[-2:]
    for q in range(2):
        cols = jnp.concatenate([d[...] for d in dy[8 * q : 8 * q + 8]], axis=0)
        out = nn(act_t[...], cols).astype(BF)
        out_own[q] = out[:F]
        out_oth[q] = out[F:]


def down_call(scalars, act_t, dy, behind):
    cols = [pl.BlockSpec((ROWS, 256), lambda i, s, q=q: (0, s[9 + 2 * i + q])) for q in range(2)]
    return pl.pallas_call(
        down_kernel,
        grid_spec=pltpu.PrefetchScalarGridSpec(
            num_scalar_prefetch=1,
            grid=(4,),
            in_specs=[pl.BlockSpec((2 * F, 8 * ROWS), lambda i, s: (0, 0))]
            + [cols[0]] * 8
            + [cols[1]] * 8
            + [ANY] * len(behind),
            out_specs=[pl.BlockSpec((2, F, 256), lambda i, s: (i, 0, 0))] * 2,
        ),
        out_shape=[struct(8, F, 256)] * 2,
        compiler_params=params(),
        cost_estimate=cost(),
        name="down",
    )(scalars, act_t, *dy, *dy, *behind)


def weight_kernel(s_ref, gda, gdb, uda, udb, *refs):
    out_own, out_oth, out_gain = refs[-3:]
    for q in range(2):
        unit, gain, wgo, wuo, wgx, wux = refs[6 * q : 6 * q + 6]
        low = jnp.concatenate([unit[s_ref[p]] for p in range(4)], axis=1)
        high = jnp.concatenate([unit[s_ref[p]] for p in range(4, 8)], axis=1)
        scale = gain[...]
        total = jnp.zeros((256, 128), F32)
        for da, db, at, w_own, w_oth in (
            (gda, gdb, 0, wgo[...], wgx[0]),
            (uda, udb, F, wuo[...], wux[0]),
        ):
            for half, w, out in ((0, w_own, out_own), (F, w_oth, out_oth)):
                grad = nn(low, da[:, half : half + F]) + nn(high, db[:, half : half + F])
                out[q, :, at : at + F] = (grad * scale).astype(BF)
                prod = grad * w.astype(F32)
                for k in range(4):
                    total = total + prod[:, k * 128 : (k + 1) * 128]
        out_gain[q] = total


def weight_call(scalars, deltas, unit, gain, own, other, behind):
    full = pl.BlockSpec((4 * ROWS, 2 * F), lambda i, s: (0, 0))
    specs, args = [full] * 4, list(deltas)
    for q in range(2):
        at = lambda i, s, q=q: (s[9 + 2 * i + q], 0)
        specs.append(pl.BlockSpec((8, 256, ROWS), lambda i, s, q=q: (0, s[9 + 2 * i + q], 0)))
        specs += [pl.BlockSpec((256, 1), at)] + [pl.BlockSpec((256, F), at)] * 2
        for k in (1, 2):
            specs.append(pl.BlockSpec((1, 256, F), lambda i, s, q=q, k=k: (s[9 + 2 * i + q], k, 0)))
        args += [unit, gain, *own, *other]
    specs += [ANY] * len(behind)
    args += behind
    return pl.pallas_call(
        weight_kernel,
        grid_spec=pltpu.PrefetchScalarGridSpec(
            num_scalar_prefetch=1,
            grid=(4,),
            in_specs=specs,
            out_specs=[pl.BlockSpec((2, 256, 2 * F), lambda i, s: (i, 0, 0))] * 2
            + [pl.BlockSpec((2, 256, 128), lambda i, s: (i, 0, 0))],
        ),
        out_shape=[struct(8, 256, 2 * F)] * 2 + [struct(8, 256, 128, dtype=F32)],
        compiler_params=params(),
        cost_estimate=cost(),
        name="weights",
    )(scalars, *args)


def last_kernel(tokens, dy, gain, own, a, b, e, f, out):
    x = tokens[...].astype(F32)
    inverse = lax.rsqrt(jnp.mean(x * x, axis=-1, keepdims=True) + 1e-05)
    unit = x * inverse
    normed_grad = total_of(own[...], a[0], b[0], e[...], f[...])
    scaled = gain[...] * normed_grad
    mean_term = jnp.mean(scaled * unit, axis=-1, keepdims=True)
    out[...] = (dy[...].astype(F32) + inverse * (scaled - unit * mean_term)).astype(BF)


def last_call(tokens, dy, gain, own, a, b, e, f):
    rows = pl.BlockSpec((32, D), lambda i: (i, 0))
    first = pl.BlockSpec((1, 32, D), lambda i: (0, i, 0))
    return pl.pallas_call(
        last_kernel,
        grid=(4,),
        in_specs=[rows, rows, pl.BlockSpec((1, D), lambda i: (0, 0)), rows, first, first, rows, rows],
        out_specs=rows,
        out_shape=struct(ROWS, D),
        compiler_params=params(),
        cost_estimate=cost(),
        name="last",
    )(tokens, dy, gain, own, a, b, e, f)


def total_of(*terms):
    out = terms[0].astype(F32)
    for term in terms[1:]:
        out = out + term.astype(F32)
    return out


def pair_sums(own, back):
    return [total_of(own[2 * r : 2 * r + 2], back[2 * r : 2 * r + 2]) for r in range(4)]


def along_x(parts):
    return [send(parts[r].astype(BF), x=r) for r in (1, 2, 3)]


def local(tokens, gain, gate_saved, up_saved, out_grad, gate_weight, up_weight, down_weight):
    zh, x_at, zl, y, c = (lax.axis_index(a) for a in AXES)
    oz = 1 - zl
    near = [zl * 4 + (y + k) % 4 for k in (0, 3, 1, 2)]
    far = [oz * 4 + (y + k) % 4 for k in (0, 3, 1, 2)]
    places = [near[0], far[0], near[1], near[2], near[3], far[1], far[2], far[3]]
    order = [((zh + q) % 2) * 4 + (x_at + r) % 4 for r in range(4) for q in range(2)]
    scalars = jnp.stack(places + [c] + order).astype(jnp.int32)

    d_z = send(out_grad, zl=1)
    d_2 = send(out_grad, y=2)
    d_m = send(out_grad, y=1)
    d_p = send(out_grad, y=-1)
    gate4 = gate_saved.reshape(8, 2, ROWS, F)
    up4 = up_saved.reshape(8, 2, ROWS, F)
    unit_t, pack = first_call(scalars, tokens, gate4, up4, gate_weight, up_weight, down_weight)
    pack = send(pack, c=1)
    weights = (down_weight, gate_weight, up_weight, pack)

    d_zm = send(d_z, y=1)
    d_zp = send(d_z, y=-1)
    d_z2 = send(d_2, zl=1)
    unit = lax.all_gather(after(unit_t, d_m, d_p, d_zm, d_zp, d_z2), ("zl", "y"), axis=0, tiled=False)
    *factors, act_t = factor_call(scalars, gate4, up4, pack)
    dy_a = (out_grad, d_z, d_m, d_p)
    dy_b = (d_2, d_zm, d_zp, d_z2)
    gd_a, ud_a, n_own, n_z, ym, yp = delta_call(False, dy_a, factors, weights)
    down_own, down_oth = down_call(scalars, act_t, dy_a + dy_b, (gd_a,))
    gd_b, ud_b, n_2, n_ym, n_yp, n_z2 = delta_call(
        True, dy_b, factors, weights, (ym, yp), (down_oth,)
    )
    down_back = send(down_oth, c=1)
    parts = pair_sums(down_own, after(down_back, gd_b))
    down_got = along_x(parts)
    a = send(n_yp, y=1)
    b = send(n_ym, y=-1)

    w_own, w_oth, gain_part = weight_call(
        scalars,
        (gd_a, gd_b, ud_a, ud_b),
        unit,
        gain.reshape(D, 1),
        (gate_weight, up_weight),
        (pack, pack),
        [down_back],
    )
    gain_rows = jnp.sum(gain_part, axis=-1).reshape(4, 2, 256)
    gain_rows = jnp.roll(gain_rows, (x_at, zh), (0, 1)).transpose(1, 0, 2).reshape(16, 128)
    w_back = send(after(w_oth, a, b, *down_got), c=1)
    gain_rows = total_of(gain_rows, *(send(gain_rows, x=r) for r in (1, 2, 3)))
    w_parts = pair_sums(w_own, after(w_back, gain_rows))
    w_got = along_x(w_parts)
    down_both = total_of(parts[0], *down_got)
    down_last = send(down_both[1].astype(BF), zh=1)
    d = send(n_z2, zl=1)
    e = send(total_of(n_2, d).astype(BF), y=2)
    f = send(total_of(n_z, a[1], b[1]).astype(BF), zl=1)
    for shift in ({"zh": 1}, {"c": 1}, {"zl": 1}, {"y": 1}, {"y": 2}):
        gain_rows = gain_rows + send(gain_rows, **shift)
    token_grad = last_call(tokens, out_grad, gain.reshape(1, D), n_own, a, b, e, f)

    w_both = total_of(w_parts[0], *(after(g, gain_rows, token_grad) for g in w_got))
    both_sum = w_both[0] + send(w_both[1].astype(BF), zh=1).astype(F32)
    return (
        token_grad,
        gain_rows.reshape(D),
        both_sum[:, :F].astype(BF),
        both_sum[:, F:].astype(BF),
        (down_both[0] + down_last.astype(F32)).astype(BF),
    )


def solution(mesh):
    mesh = Mesh(mesh.devices.reshape(SIZES), AXES)
    dp, tensor = ("zh", "x"), ("zl", "y", "c")
    placed = (
        P(dp + tensor, None),
        P(),
        P(dp, tensor),
        P(dp, tensor),
        P(dp + tensor, None),
        P(None, tensor),
        P(None, tensor),
        P(tensor, None),
    )
    return jax.shard_map(
        local,
        mesh=mesh,
        in_specs=placed,
        out_specs=(
            P(dp + tensor, None),
            P(),
            P(dp, tensor),
            P(dp, tensor),
            P(tensor, dp),
        ),
        check_vma=False,
    )
```

```python
import functools

import jax
import jax.numpy as jnp
import numpy as np
from jax import lax
from jax.experimental import pallas as pl
from jax.experimental.pallas import tpu as pltpu
from jax.sharding import Mesh, PartitionSpec as P

AXES = ("zh", "x", "zl", "y", "c")
SIZES = (2, 4, 2, 4, 2)
D = 2048
ROWS = 128
F = 512
BF = jnp.bfloat16
F32 = jnp.float32
MIB = 1024 * 1024
ANY = pl.BlockSpec(memory_space=pl.ANY)


def send(value, **shift):
    ids = np.arange(128).reshape(SIZES)
    pairs = []
    for at in np.ndindex(*SIZES):
        to = tuple((a + shift.get(n, 0)) % s for a, n, s in zip(at, AXES, SIZES))
        pairs.append((int(ids[at]), int(ids[to])))
    return lax.ppermute(value, AXES, pairs)


def nt(a, b):
    return lax.dot_general(a, b, (((1,), (1,)), ((), ())), preferred_element_type=F32)


def nn(a, b):
    return lax.dot_general(a, b, (((1,), (0,)), ((), ())), preferred_element_type=F32)


def struct(*shape, dtype=BF):
    return jax.ShapeDtypeStruct(shape, dtype)


def params():
    return pltpu.CompilerParams(vmem_limit_bytes=60 * MIB)


def cost(mults=0):
    return pl.CostEstimate(flops=2 * mults + 1024, bytes_accessed=1024, transcendentals=0)


def after(value, *others):
    return lax.optimization_barrier((value, *others))[0]


def first_kernel(s_ref, tokens, gain, gate, up, wg, wu, wd, normed_t, pack):
    @pl.when(pl.program_id(0) == 0)
    def _():
        x = tokens[...].astype(F32)
        unit = x * lax.rsqrt(jnp.mean(x * x, axis=-1, keepdims=True) + 1e-05)
        normed_t[...] = (unit * gain[...]).astype(BF).T

    for j in range(2):
        pack[j, :128] = gate[j, 0]
        pack[j, 128:256] = up[j, 0]
        pack[j, 256:512] = wg[j * 256 : j * 256 + 256]
        pack[j, 512:768] = wu[j * 256 : j * 256 + 256]
        for k in range(4):
            at = 768 + k * 64
            pack[j, at : at + 64] = wd[j * 64 : j * 64 + 64, k * F : k * F + F]


def first_call(scalars, tokens, gain, gate4, up4, wg, wu, wd):
    half = pl.BlockSpec((2, 1, ROWS, F), lambda i, s: (i, 1 - s[8], 0, 0))
    rows = pl.BlockSpec((512, F), lambda i, s: (i, 0))
    return pl.pallas_call(
        first_kernel,
        grid_spec=pltpu.PrefetchScalarGridSpec(
            num_scalar_prefetch=1,
            grid=(4,),
            in_specs=[
                pl.BlockSpec((ROWS, D), lambda i, s: (0, 0)),
                pl.BlockSpec((1, D), lambda i, s: (0, 0)),
                half,
                half,
                rows,
                rows,
                pl.BlockSpec((128, D), lambda i, s: (i, 0)),
            ],
            out_specs=[
                pl.BlockSpec((D, ROWS), lambda i, s: (0, 0)),
                pl.BlockSpec((2, 1024, F), lambda i, s: (i, 0, 0)),
            ],
        ),
        out_shape=[struct(D, ROWS), struct(8, 1024, F)],
        compiler_params=params(),
        cost_estimate=cost(),
        name="first",
    )(scalars, tokens, gain, gate4, up4, wg, wu, wd)


def factor_kernel(s_ref, gate, up, for_gate, for_up, act_t):
    g = gate[...].astype(F32)
    u = up[...].astype(F32)
    sigma = 0.5 + 0.5 * jnp.tanh(0.5 * g)
    silu = g * sigma
    for_up[...] = silu.astype(BF)
    for_gate[...] = (u * sigma * (1.0 + g * (1.0 - sigma))).astype(BF)
    act_t[...] = (silu * u).astype(BF).T


def factor_call(scalars, gate, up, other):
    if other:
        specs = [pl.BlockSpec((None, ROWS, F), lambda i, s, k=k: (s[i], k, 0)) for k in range(2)]
    else:
        specs = [pl.BlockSpec((None, None, ROWS, F), lambda i, s: (s[i], s[8], 0, 0))] * 2
    rows = pl.BlockSpec((ROWS, F), lambda i, s: (i, 0))
    return pl.pallas_call(
        factor_kernel,
        grid_spec=pltpu.PrefetchScalarGridSpec(
            num_scalar_prefetch=1,
            grid=(8,),
            in_specs=specs,
            out_specs=[rows, rows, pl.BlockSpec((F, ROWS), lambda i, s: (0, i))],
        ),
        out_shape=[struct(8 * ROWS, F)] * 2 + [struct(F, 8 * ROWS)],
        compiler_params=params(),
        cost_estimate=cost(),
        name="factors_other" if other else "factors_own",
    )(scalars, gate, up)


def delta_body(dy, factors, weights, gd, ud, outs, held, sem):
    wd, wg, wu, pack = weights
    wd_own, wd_oth, wg_own, wg_oth, wu_own, wu_oth = held
    moves = ((wd, wd_own), (pack.at[:, 768:1024], wd_oth), (wg, wg_own))
    moves += ((pack.at[:, 256:512], wg_oth), (wu, wu_own), (pack.at[:, 512:768], wu_oth))
    copies = [pltpu.make_async_copy(a, b, sem.at[k]) for k, (a, b) in enumerate(moves)]
    for copy in copies:
        copy.start()
    rows = jnp.concatenate(dy, axis=0)

    def store(hidden, at):
        for_gate, for_up = factors[2:] if at.start else factors[:2]
        gd[:, at] = (hidden * for_gate[...].astype(F32)).astype(BF)
        ud[:, at] = (hidden * for_up[...].astype(F32)).astype(BF)

    copies[0].wait()
    store(nt(rows, wd_own[...]), slice(0, F))
    copies[1].wait()
    hidden = 0
    for k in range(4):
        block = wd_oth[:, k * 64 : k * 64 + 64, :].reshape(F, F)
        hidden = hidden + nt(rows[:, k * F : k * F + F], block)
    store(hidden, slice(F, 2 * F))
    for copy in copies[2:]:
        copy.wait()
    for n in range(4):
        at, two = slice(n * 512, n * 512 + 512), slice(2 * n, 2 * n + 2)
        out = nt(gd[:, :F], wg_own[at, :])
        out = out + nt(gd[:, F:], wg_oth[two].reshape(F, F))
        out = out + nt(ud[:, :F], wu_own[at, :])
        out = (out + nt(ud[:, F:], wu_oth[two].reshape(F, F))).astype(BF)
        for k, ref in enumerate(outs):
            ref[:, at] = out[k * ROWS : k * ROWS + ROWS]


def delta_kernel_a(*refs):
    dy = [r[...] for r in refs[:4]]
    gd, ud, *outs = refs[-13:-7]
    delta_body(dy, refs[4:8], refs[8:12], gd, ud, outs, refs[-7:-1], refs[-1])


def delta_kernel_b(*refs):
    dy = [r[k] for r in refs[:2] for k in range(2)]
    gd, ud, ym, yp = refs[-11:-7]
    outs = (ym.at[0], ym.at[1], yp.at[0], yp.at[1])
    delta_body(dy, refs[2:6], refs[6:10], gd, ud, outs, refs[-7:-1], refs[-1])


def delta_call(second, dy, factors, weights, behind=()):
    at = 1 if second else 0
    wide = pl.BlockSpec((4 * ROWS, F), lambda i: (at, 0))
    here = pl.BlockSpec((4 * ROWS, 2 * F), lambda i: (0, 0))
    if second:
        count, piece = 2, struct(2, ROWS, D)
        spec = pl.BlockSpec((2, ROWS, D), lambda i: (0, 0, 0))
    else:
        count, piece = 4, struct(ROWS, D)
        spec = pl.BlockSpec((ROWS, D), lambda i: (0, 0))
    return pl.pallas_call(
        delta_kernel_b if second else delta_kernel_a,
        grid=(1,),
        in_specs=[spec] * count + [wide] * 4 + [ANY] * 4 + [ANY] * len(behind),
        out_specs=[here, here] + [spec] * count,
        out_shape=[struct(4 * ROWS, 2 * F)] * 2 + [piece] * count,
        scratch_shapes=[pltpu.VMEM((F, D), BF), pltpu.VMEM((8, 256, F), BF)]
        + [pltpu.VMEM((D, F), BF), pltpu.VMEM((8, 256, F), BF)] * 2
        + [pltpu.SemaphoreType.DMA((6,))],
        compiler_params=params(),
        cost_estimate=cost(),
        name="deltas_b" if second else "deltas_a",
    )(*dy, *factors, *weights, *behind)


def down_kernel(s_ref, act_own, act_oth, *refs):
    out_own, out_oth = refs[-2:]
    for q in range(2):
        dy = refs[6 * q : 6 * q + 6]
        cols = [d[...] for d in dy[:4]] + [d[k] for d in dy[4:] for k in range(2)]
        cols = jnp.concatenate(cols, axis=0)
        out_own[q] = nn(act_own[...], cols).astype(BF)
        out_oth[q] = nn(act_oth[...], cols).astype(BF)


def down_call(scalars, acts, dy, behind):
    specs = [pl.BlockSpec((F, 8 * ROWS), lambda i, s: (0, 0))] * 2
    for q in range(2):
        specs += [pl.BlockSpec((ROWS, 256), lambda i, s, q=q: (0, s[9 + 2 * i + q]))] * 4
        specs += [pl.BlockSpec((2, ROWS, 256), lambda i, s, q=q: (0, 0, s[9 + 2 * i + q]))] * 2
    return pl.pallas_call(
        down_kernel,
        grid_spec=pltpu.PrefetchScalarGridSpec(
            num_scalar_prefetch=1,
            grid=(4,),
            in_specs=specs + [ANY] * len(behind),
            out_specs=[pl.BlockSpec((2, F, 256), lambda i, s: (i, 0, 0))] * 2,
        ),
        out_shape=[struct(8, F, 256)] * 2,
        compiler_params=params(),
        cost_estimate=cost(),
        name="down",
    )(scalars, *acts, *dy, *dy, *behind)


def weight_kernel(s_ref, gda, gdb, uda, udb, *refs):
    out_own, out_oth, out_gain = refs[-3:]
    for q in range(2):
        unit, (wgo, wuo, wgx, wux) = refs[10 * q : 10 * q + 6], refs[10 * q + 6 : 10 * q + 10]
        low = jnp.concatenate([u[...] for u in unit[:4]], axis=1)
        high = jnp.concatenate([u[k] for u in unit[4:] for k in range(2)], axis=1)
        total = jnp.zeros((256, 128), F32)
        for da, db, at, w_own, w_oth in (
            (gda, gdb, 0, wgo[...], wgx[0]),
            (uda, udb, F, wuo[...], wux[0]),
        ):
            for half, w, out in ((0, w_own, out_own), (F, w_oth, out_oth)):
                grad = nn(low, da[:, half : half + F]) + nn(high, db[:, half : half + F])
                out[q, :, at : at + F] = grad.astype(BF)
                prod = grad * w.astype(F32)
                for k in range(4):
                    total = total + prod[:, k * 128 : (k + 1) * 128]
        out_gain[q] = total


def weight_call(places, scalars, deltas, unit, own, pack, behind):
    count = len(places)
    step = places[1] - places[0] if count > 1 else 0

    def row(i, s, q):
        return s[9 + 2 * (places[0] + step * i) + q]

    full = pl.BlockSpec((4 * ROWS, 2 * F), lambda i, s: (0, 0))
    specs, args = [full] * 4, list(deltas)
    for q in range(2):
        at = lambda i, s, q=q: (row(i, s, q), 0)
        specs += [pl.BlockSpec((256, ROWS), at)] * 4
        specs += [pl.BlockSpec((2, 256, ROWS), lambda i, s, q=q: (0, row(i, s, q), 0))] * 2
        specs += [pl.BlockSpec((256, F), at)] * 2
        for k in (1, 2):
            specs.append(pl.BlockSpec((1, 256, F), lambda i, s, q=q, k=k: (row(i, s, q), k, 0)))
        args += [*unit, *own, pack, pack]
    specs += [ANY] * len(behind)
    args += behind
    return pl.pallas_call(
        weight_kernel,
        grid_spec=pltpu.PrefetchScalarGridSpec(
            num_scalar_prefetch=1,
            grid=(count,),
            in_specs=specs,
            out_specs=[pl.BlockSpec((2, 256, 2 * F), lambda i, s: (i, 0, 0))] * 2
            + [pl.BlockSpec((2, 256, 128), lambda i, s: (i, 0, 0))],
        ),
        out_shape=[struct(2 * count, 256, 2 * F)] * 2 + [struct(2 * count, 256, 128, dtype=F32)],
        compiler_params=params(),
        cost_estimate=cost(),
        name="weights_" + "_".join(str(r) for r in places),
    )(scalars, *args)


def last_kernel(tokens, dy, gain, own, a, b, e, f, *refs):
    x = tokens[...].astype(F32)
    inverse = lax.rsqrt(jnp.mean(x * x, axis=-1, keepdims=True) + 1e-05)
    unit = x * inverse
    normed_grad = total_of(own[...], a[0], b[0], e[...], f[...])
    scaled = gain[...] * normed_grad
    mean_term = jnp.mean(scaled * unit, axis=-1, keepdims=True)
    refs[-1][...] = (dy[...].astype(F32) + inverse * (scaled - unit * mean_term)).astype(BF)


def last_call(tokens, dy, gain, own, a, b, e, f, behind):
    rows = pl.BlockSpec((32, D), lambda i: (i, 0))
    first = pl.BlockSpec((1, 32, D), lambda i: (0, i, 0))
    return pl.pallas_call(
        last_kernel,
        grid=(4,),
        in_specs=[rows, rows, pl.BlockSpec((1, D), lambda i: (0, 0)), rows, first, first, rows, rows]
        + [ANY] * len(behind),
        out_specs=rows,
        out_shape=struct(ROWS, D),
        compiler_params=params(),
        cost_estimate=cost(),
        name="last",
    )(tokens, dy, gain, own, a, b, e, f, *behind)


def total_of(*terms):
    out = terms[0].astype(F32)
    for term in terms[1:]:
        out = out + term.astype(F32)
    return out


def sum_call(body, own, back, behind, out_specs, out_shape, name):
    block = pl.BlockSpec((2, *own.shape[1:]), lambda i: (i, 0, 0))
    return pl.pallas_call(
        body,
        grid=(own.shape[0] // 2,),
        in_specs=[block, block] + [ANY] * len(behind),
        out_specs=out_specs,
        out_shape=out_shape,
        compiler_params=params(),
        cost_estimate=cost(),
        name=name,
    )(own, back, *behind)


def pair_sums(own, back, behind=()):
    count, rows, cols = own.shape

    def body(own, back, *refs):
        total = total_of(own[...], back[...]).astype(BF)
        for r, out in enumerate(refs[len(behind) :]):

            @pl.when(pl.program_id(0) == r)
            def _():
                out[...] = total

    specs = [pl.BlockSpec((2, rows, cols), lambda i: (0, 0, 0))] * (count // 2)
    shapes = [struct(2, rows, cols)] * (count // 2)
    return sum_call(body, own, back, behind, specs, shapes, "pair_sums")


def split_sums(own, back, behind=()):
    count, rows, cols = own.shape
    half = rows // 2

    def body(own, back, *refs):
        refs = refs[len(behind) :]
        total = total_of(own[...], back[...]).astype(BF)
        for r, out in enumerate(refs[:-2]):

            @pl.when(pl.program_id(0) == r)
            def _():
                out[...] = total[:, :half]

        for q, out in enumerate(refs[-2:]):
            out[0] = total[q, half:]

    specs = [pl.BlockSpec((2, half, cols), lambda i: (0, 0, 0))] * (count // 2)
    specs += [pl.BlockSpec((1, half, cols), lambda i: (i, 0, 0))] * 2
    shapes = [struct(2, half, cols)] * (count // 2) + [struct(count // 2, half, cols)] * 2
    return sum_call(body, own, back, behind, specs, shapes, "split_sums")


def local(tokens, gain, gate_saved, up_saved, out_grad, gate_weight, up_weight, down_weight):
    zh, x_at, zl, y, c = (lax.axis_index(a) for a in AXES)
    near = [zl * 4 + (y + k) % 4 for k in (0, 2, 3, 1)]
    far = [(1 - zl) * 4 + (y + k) % 4 for k in (0, 2, 3, 1)]
    places = [p for pair in zip(near, far) for p in pair]
    order = [((zh + q) % 2) * 4 + (x_at + r) % 4 for r in range(4) for q in range(2)]
    scalars = jnp.stack(places + [c] + order).astype(jnp.int32)

    d_z = send(out_grad, zl=1)
    d_2 = send(out_grad, y=2)
    gate4 = gate_saved.reshape(8, 2, ROWS, F)
    up4 = up_saved.reshape(8, 2, ROWS, F)
    normed_t, pack = first_call(
        scalars, tokens, gain.reshape(1, D), gate4, up4, gate_weight, up_weight, down_weight
    )
    pack = send(after(pack, d_z, d_2), c=1)
    weights = (down_weight, gate_weight, up_weight, pack)

    d_pair = jnp.stack([out_grad, after(d_z, d_2)])
    d_m = send(d_pair, y=1)
    d_p = send(d_pair, y=-1)
    d_z2 = send(d_2, zl=1)
    *factors, act_own = factor_call(scalars, after(gate4, d_pair), up4, False)
    normed_b = after(normed_t, pack, act_own)
    u_z = send(normed_b, zl=1)
    u_2 = send(normed_b, y=2)
    *others, act_oth = factor_call(scalars, pack, pack, True)
    factors += others
    dy_a, dy_b = (out_grad, d_z, d_2, d_z2), (d_m, d_p)
    gd_a, ud_a, n_own, n_z, n_2, n_z2 = delta_call(False, dy_a, factors, weights)
    u_pair = jnp.stack([normed_t, after(u_z, u_2, gd_a)])
    u_m = send(u_pair, y=1)
    u_p = send(u_pair, y=-1)
    u_z2 = send(after(u_2, gd_a), zl=1)
    down_own, down_oth = down_call(
        scalars, (act_own, act_oth), dy_a + dy_b, (gd_a, u_pair, u_2)
    )
    down_back = send(down_oth, c=1)
    gd_b, ud_b, n_ym, n_yp = delta_call(True, dy_b, factors, weights, (down_oth,))
    parts = pair_sums(down_own, down_back, (gd_b, u_z2))
    down_got = [send(parts[r], x=r) for r in (1, 2, 3)]
    a = send(n_yp, y=1)
    b = send(n_ym, y=-1)
    d = send(n_z2, zl=1)

    w_args = (
        scalars,
        (gd_a, gd_b, ud_a, ud_b),
        (normed_t, u_z, u_2, u_z2, u_m, u_p),
        (gate_weight, up_weight),
        pack,
    )
    own_0, oth_0, gain_0 = weight_call((0,), *w_args, [parts[0], d])
    own_r, oth_r, gain_r = weight_call((1, 2, 3), *w_args, [own_0])
    back_r = send(after(oth_r, a, b, *down_got), c=1)
    f = send(total_of(after(n_z, oth_r), a[1], b[1]).astype(BF), zl=1)
    *up_r, low_same, low_other = split_sums(own_r, back_r)
    up_got = [send(up_r[r - 1], x=r) for r in (1, 2, 3)]
    low_got = send(low_other, zh=1)
    back_0 = send(after(oth_0, low_other), c=1)
    part_0 = total_of(own_0, back_0)
    down_both = total_of(parts[0], *(after(g, low_other) for g in down_got))
    down_last = send(down_both[1].astype(BF), zh=1)
    e = send(total_of(n_2, after(d, low_other)).astype(BF), y=2)
    token_grad = last_call(tokens, out_grad, gain.reshape(1, D), n_own, a, b, e, f, ())

    gain_rows = jnp.concatenate([jnp.sum(g, axis=-1) for g in (gain_0, gain_r)])
    gain_rows = jnp.roll(gain_rows.reshape(4, 2, 256), (x_at, zh), (0, 1))
    gain_rows = gain_rows.transpose(1, 0, 2).reshape(D)
    gain_rows = gain_rows.reshape(16, 128)
    low_sum = total_of(low_same, low_got)
    low_x = [send(low_sum[r - 1].astype(BF), x=r) for r in (1, 2, 3)]
    up_got = [after(g, token_grad) for g in up_got]
    up_sum = total_of(part_0[:, :128], *up_got)
    rest = send(jnp.concatenate([up_sum[1], part_0[1, 128:]]).astype(BF), zh=1).astype(F32)
    gain_rows = after(gain_rows, *up_got)
    for shift in ({"c": 1}, {"y": 1}, {"y": 2}, {"zl": 1}, {"zh": 1}):
        gain_rows = gain_rows + send(gain_rows, **shift)
    gain_rows = after(gain_rows, *low_x)
    gain_rows = total_of(gain_rows, *(send(gain_rows, x=k) for k in (1, 2, 3)))
    gain_rows = gain_rows.reshape(D) / gain
    low_all = total_of(part_0[0, 128:] + rest[128:], *low_x)
    both_sum = jnp.concatenate([up_sum[0] + rest[:128], low_all])
    return (
        token_grad,
        gain_rows,
        both_sum[:, :F].astype(BF),
        both_sum[:, F:].astype(BF),
        (down_both[0] + down_last.astype(F32)).astype(BF),
    )


def solution(mesh):
    mesh = Mesh(mesh.devices.reshape(SIZES), AXES)
    dp, tensor = ("zh", "x"), ("zl", "y", "c")
    placed = (
        P(dp + tensor, None),
        P(),
        P(dp, tensor),
        P(dp, tensor),
        P(dp + tensor, None),
        P(None, tensor),
        P(None, tensor),
        P(tensor, None),
    )
    return jax.shard_map(
        local,
        mesh=mesh,
        in_specs=placed,
        out_specs=(
            P(dp + tensor, None),
            P(),
            P(dp, tensor),
            P(dp, tensor),
            P(tensor, dp),
        ),
        check_vma=False,
    )
```

```python
import functools

import jax
import jax.numpy as jnp
import numpy as np
from jax import lax
from jax.experimental import pallas as pl
from jax.experimental.pallas import tpu as pltpu
from jax.sharding import Mesh, PartitionSpec as P

AXES = ("zh", "x", "zl", "y", "c")
SIZES = (2, 4, 2, 4, 2)
D = 2048
ROWS = 128
F = 512
BF = jnp.bfloat16
F32 = jnp.float32
MIB = 1024 * 1024
ANY = pl.BlockSpec(memory_space=pl.ANY)


def send(value, **shift):
    ids = np.arange(128).reshape(SIZES)
    pairs = []
    for at in np.ndindex(*SIZES):
        to = tuple((a + shift.get(n, 0)) % s for a, n, s in zip(at, AXES, SIZES))
        pairs.append((int(ids[at]), int(ids[to])))
    return lax.ppermute(value, AXES, pairs)


def nt(a, b):
    return lax.dot_general(a, b, (((1,), (1,)), ((), ())), preferred_element_type=F32)


def nn(a, b):
    return lax.dot_general(a, b, (((1,), (0,)), ((), ())), preferred_element_type=F32)


def struct(*shape, dtype=BF):
    return jax.ShapeDtypeStruct(shape, dtype)


def params():
    return pltpu.CompilerParams(vmem_limit_bytes=38 * MIB)


def cost(mults=0):
    return pl.CostEstimate(flops=2 * mults + 1024, bytes_accessed=1024, transcendentals=0)


def after(value, *others):
    return lax.optimization_barrier((value, *others))[0]


def first_kernel(s_ref, tokens, gain, gate, up, wg, wu, wd, normed_t, pack):
    @pl.when(pl.program_id(0) == 0)
    def _():
        x = tokens[...].astype(F32)
        unit = x * lax.rsqrt(jnp.mean(x * x, axis=-1, keepdims=True) + 1e-05)
        normed_t[...] = (unit * gain[...]).astype(BF).T

    for j in range(2):
        pack[j, :128] = gate[j, 0]
        pack[j, 128:256] = up[j, 0]
        pack[j, 256:512] = wg[j * 256 : j * 256 + 256]
        pack[j, 512:768] = wu[j * 256 : j * 256 + 256]
        for k in range(4):
            at = 768 + k * 64
            pack[j, at : at + 64] = wd[j * 64 : j * 64 + 64, k * F : k * F + F]


def first_call(scalars, tokens, gain, gate4, up4, wg, wu, wd):
    half = pl.BlockSpec((2, 1, ROWS, F), lambda i, s: (i, 1 - s[8], 0, 0))
    rows = pl.BlockSpec((512, F), lambda i, s: (i, 0))
    return pl.pallas_call(
        first_kernel,
        grid_spec=pltpu.PrefetchScalarGridSpec(
            num_scalar_prefetch=1,
            grid=(4,),
            in_specs=[
                pl.BlockSpec((ROWS, D), lambda i, s: (0, 0)),
                pl.BlockSpec((1, D), lambda i, s: (0, 0)),
                half,
                half,
                rows,
                rows,
                pl.BlockSpec((128, D), lambda i, s: (i, 0)),
            ],
            out_specs=[
                pl.BlockSpec((D, ROWS), lambda i, s: (0, 0)),
                pl.BlockSpec((2, 1024, F), lambda i, s: (i, 0, 0)),
            ],
        ),
        out_shape=[struct(D, ROWS), struct(8, 1024, F)],
        compiler_params=params(),
        cost_estimate=cost(),
        name="first",
    )(scalars, tokens, gain, gate4, up4, wg, wu, wd)


def factor_kernel(s_ref, gate, up, for_gate, for_up, act_t):
    g = gate[...].astype(F32)
    u = up[...].astype(F32)
    sigma = 0.5 + 0.5 * jnp.tanh(0.5 * g)
    silu = g * sigma
    for_up[...] = silu.astype(BF)
    for_gate[...] = (u * sigma * (1.0 + g * (1.0 - sigma))).astype(BF)
    act_t[...] = (silu * u).astype(BF).T


def factor_call(scalars, gate, up, other):
    if other:
        specs = [pl.BlockSpec((None, ROWS, F), lambda i, s, k=k: (s[i], k, 0)) for k in range(2)]
    else:
        specs = [pl.BlockSpec((None, None, ROWS, F), lambda i, s: (s[i], s[8], 0, 0))] * 2
    rows = pl.BlockSpec((ROWS, F), lambda i, s: (i, 0))
    return pl.pallas_call(
        factor_kernel,
        grid_spec=pltpu.PrefetchScalarGridSpec(
            num_scalar_prefetch=1,
            grid=(8,),
            in_specs=specs,
            out_specs=[rows, rows, pl.BlockSpec((F, ROWS), lambda i, s: (0, i))],
        ),
        out_shape=[struct(8 * ROWS, F)] * 2 + [struct(F, 8 * ROWS)],
        compiler_params=params(),
        cost_estimate=cost(),
        name="factors_other" if other else "factors_own",
    )(scalars, gate, up)


def delta_body(dy, factors, weights, gd, ud, outs, held, sem):
    wd, wg, wu, pack = weights
    wd_own, wd_oth, wg_own, wg_oth, wu_own, wu_oth = held
    moves = ((wd, wd_own), (pack.at[:, 768:1024], wd_oth), (wg, wg_own))
    moves += ((pack.at[:, 256:512], wg_oth), (wu, wu_own), (pack.at[:, 512:768], wu_oth))
    copies = [pltpu.make_async_copy(a, b, sem.at[k]) for k, (a, b) in enumerate(moves)]
    for copy in copies:
        copy.start()
    rows = jnp.concatenate(dy, axis=0)

    def store(hidden, at):
        for_gate, for_up = factors[2:] if at.start else factors[:2]
        gd[:, at] = (hidden * for_gate[...].astype(F32)).astype(BF)
        ud[:, at] = (hidden * for_up[...].astype(F32)).astype(BF)

    copies[0].wait()
    store(nt(rows, wd_own[...]), slice(0, F))
    copies[1].wait()
    hidden = 0
    for k in range(4):
        block = wd_oth[:, k * 64 : k * 64 + 64, :].reshape(F, F)
        hidden = hidden + nt(rows[:, k * F : k * F + F], block)
    store(hidden, slice(F, 2 * F))
    for copy in copies[2:]:
        copy.wait()
    for n in range(4):
        at, two = slice(n * 512, n * 512 + 512), slice(2 * n, 2 * n + 2)
        out = nt(gd[:, :F], wg_own[at, :])
        out = out + nt(gd[:, F:], wg_oth[two].reshape(F, F))
        out = out + nt(ud[:, :F], wu_own[at, :])
        out = (out + nt(ud[:, F:], wu_oth[two].reshape(F, F))).astype(BF)
        for k, ref in enumerate(outs):
            ref[:, at] = out[k * ROWS : k * ROWS + ROWS]


def delta_kernel_a(*refs):
    dy = [r[...] for r in refs[:4]]
    gd, ud, *outs = refs[-13:-7]
    delta_body(dy, refs[4:8], refs[8:12], gd, ud, outs, refs[-7:-1], refs[-1])


def delta_kernel_b(*refs):
    dy = [r[k] for r in refs[:2] for k in range(2)]
    gd, ud, ym, yp = refs[-11:-7]
    outs = (ym.at[0], ym.at[1], yp.at[0], yp.at[1])
    delta_body(dy, refs[2:6], refs[6:10], gd, ud, outs, refs[-7:-1], refs[-1])


def delta_call(second, dy, factors, weights, behind=()):
    at = 1 if second else 0
    wide = pl.BlockSpec((4 * ROWS, F), lambda i: (at, 0))
    here = pl.BlockSpec((4 * ROWS, 2 * F), lambda i: (0, 0))
    if second:
        count, piece = 2, struct(2, ROWS, D)
        spec = pl.BlockSpec((2, ROWS, D), lambda i: (0, 0, 0))
    else:
        count, piece = 4, struct(ROWS, D)
        spec = pl.BlockSpec((ROWS, D), lambda i: (0, 0))
    return pl.pallas_call(
        delta_kernel_b if second else delta_kernel_a,
        grid=(1,),
        in_specs=[spec] * count + [wide] * 4 + [ANY] * 4 + [ANY] * len(behind),
        out_specs=[here, here] + [spec] * count,
        out_shape=[struct(4 * ROWS, 2 * F)] * 2 + [piece] * count,
        scratch_shapes=[pltpu.VMEM((F, D), BF), pltpu.VMEM((8, 256, F), BF)]
        + [pltpu.VMEM((D, F), BF), pltpu.VMEM((8, 256, F), BF)] * 2
        + [pltpu.SemaphoreType.DMA((6,))],
        compiler_params=params(),
        cost_estimate=cost(),
        name="deltas_b" if second else "deltas_a",
    )(*dy, *factors, *weights, *behind)


def down_kernel(s_ref, act_own, act_oth, *refs):
    out_own, out_oth = refs[-2:]
    for q in range(2):
        dy = refs[6 * q : 6 * q + 6]
        cols = [d[...] for d in dy[:4]] + [d[k] for d in dy[4:] for k in range(2)]
        cols = jnp.concatenate(cols, axis=0)
        out_own[q] = nn(act_own[...], cols).astype(BF)
        out_oth[q] = nn(act_oth[...], cols).astype(BF)


def down_call(scalars, acts, dy, behind):
    specs = [pl.BlockSpec((F, 8 * ROWS), lambda i, s: (0, 0))] * 2
    for q in range(2):
        specs += [pl.BlockSpec((ROWS, 256), lambda i, s, q=q: (0, s[9 + 2 * i + q]))] * 4
        specs += [pl.BlockSpec((2, ROWS, 256), lambda i, s, q=q: (0, 0, s[9 + 2 * i + q]))] * 2
    return pl.pallas_call(
        down_kernel,
        grid_spec=pltpu.PrefetchScalarGridSpec(
            num_scalar_prefetch=1,
            grid=(4,),
            in_specs=specs + [ANY] * len(behind),
            out_specs=[pl.BlockSpec((2, F, 256), lambda i, s: (i, 0, 0))] * 2,
        ),
        out_shape=[struct(8, F, 256)] * 2,
        compiler_params=params(),
        cost_estimate=cost(),
        name="down",
    )(scalars, *acts, *dy, *dy, *behind)


def weight_kernel(s_ref, gda, gdb, uda, udb, *refs):
    out_own, out_oth, out_gain = refs[-3:]
    for q in range(2):
        unit, (wgo, wuo, wgx, wux) = refs[10 * q : 10 * q + 6], refs[10 * q + 6 : 10 * q + 10]
        low = jnp.concatenate([u[...] for u in unit[:4]], axis=1)
        high = jnp.concatenate([u[k] for u in unit[4:] for k in range(2)], axis=1)
        total = jnp.zeros((256, 128), F32)
        for da, db, at, w_own, w_oth in (
            (gda, gdb, 0, wgo[...], wgx[0]),
            (uda, udb, F, wuo[...], wux[0]),
        ):
            for half, w, out in ((0, w_own, out_own), (F, w_oth, out_oth)):
                grad = nn(low, da[:, half : half + F]) + nn(high, db[:, half : half + F])
                out[q, :, at : at + F] = grad.astype(BF)
                prod = grad * w.astype(F32)
                for k in range(4):
                    total = total + prod[:, k * 128 : (k + 1) * 128]
        out_gain[q] = total


def weight_call(places, scalars, deltas, unit, own, pack, behind):
    count = len(places)
    step = places[1] - places[0] if count > 1 else 0

    def row(i, s, q):
        return s[9 + 2 * (places[0] + step * i) + q]

    full = pl.BlockSpec((4 * ROWS, 2 * F), lambda i, s: (0, 0))
    specs, args = [full] * 4, list(deltas)
    for q in range(2):
        at = lambda i, s, q=q: (row(i, s, q), 0)
        specs += [pl.BlockSpec((256, ROWS), at)] * 4
        specs += [pl.BlockSpec((2, 256, ROWS), lambda i, s, q=q: (0, row(i, s, q), 0))] * 2
        specs += [pl.BlockSpec((256, F), at)] * 2
        for k in (1, 2):
            specs.append(pl.BlockSpec((1, 256, F), lambda i, s, q=q, k=k: (row(i, s, q), k, 0)))
        args += [*unit, *own, pack, pack]
    specs += [ANY] * len(behind)
    args += behind
    return pl.pallas_call(
        weight_kernel,
        grid_spec=pltpu.PrefetchScalarGridSpec(
            num_scalar_prefetch=1,
            grid=(count,),
            in_specs=specs,
            out_specs=[pl.BlockSpec((2, 256, 2 * F), lambda i, s: (i, 0, 0))] * 2
            + [pl.BlockSpec((2, 256, 128), lambda i, s: (i, 0, 0))],
        ),
        out_shape=[struct(2 * count, 256, 2 * F)] * 2 + [struct(2 * count, 256, 128, dtype=F32)],
        compiler_params=params(),
        cost_estimate=cost(),
        name="weights_" + "_".join(str(r) for r in places),
    )(scalars, *args)


def last_kernel(tokens, dy, gain, own, a, b, e, f, *refs):
    x = tokens[...].astype(F32)
    inverse = lax.rsqrt(jnp.mean(x * x, axis=-1, keepdims=True) + 1e-05)
    unit = x * inverse
    normed_grad = total_of(own[...], a[0], b[0], e[...], f[...])
    scaled = gain[...] * normed_grad
    mean_term = jnp.mean(scaled * unit, axis=-1, keepdims=True)
    refs[-1][...] = (dy[...].astype(F32) + inverse * (scaled - unit * mean_term)).astype(BF)


def last_call(tokens, dy, gain, own, a, b, e, f, behind):
    rows = pl.BlockSpec((32, D), lambda i: (i, 0))
    first = pl.BlockSpec((1, 32, D), lambda i: (0, i, 0))
    return pl.pallas_call(
        last_kernel,
        grid=(4,),
        in_specs=[rows, rows, pl.BlockSpec((1, D), lambda i: (0, 0)), rows, first, first, rows, rows]
        + [ANY] * len(behind),
        out_specs=rows,
        out_shape=struct(ROWS, D),
        compiler_params=params(),
        cost_estimate=cost(),
        name="last",
    )(tokens, dy, gain, own, a, b, e, f, *behind)


def total_of(*terms):
    out = terms[0].astype(F32)
    for term in terms[1:]:
        out = out + term.astype(F32)
    return out


def sum_call(body, own, back, behind, out_specs, out_shape, name):
    block = pl.BlockSpec((2, *own.shape[1:]), lambda i: (i, 0, 0))
    return pl.pallas_call(
        body,
        grid=(own.shape[0] // 2,),
        in_specs=[block, block] + [ANY] * len(behind),
        out_specs=out_specs,
        out_shape=out_shape,
        compiler_params=params(),
        cost_estimate=cost(),
        name=name,
    )(own, back, *behind)


def pair_sums(own, back, behind=()):
    count, rows, cols = own.shape

    def body(own, back, *refs):
        total = total_of(own[...], back[...]).astype(BF)
        for r, out in enumerate(refs[len(behind) :]):

            @pl.when(pl.program_id(0) == r)
            def _():
                out[...] = total

    specs = [pl.BlockSpec((2, rows, cols), lambda i: (0, 0, 0))] * (count // 2)
    shapes = [struct(2, rows, cols)] * (count // 2)
    return sum_call(body, own, back, behind, specs, shapes, "pair_sums")


def split_sums(own, back, behind=()):
    count, rows, cols = own.shape
    half = rows // 2

    def body(own, back, *refs):
        refs = refs[len(behind) :]
        total = total_of(own[...], back[...]).astype(BF)
        for r, out in enumerate(refs[:-2]):

            @pl.when(pl.program_id(0) == r)
            def _():
                out[...] = total[:, :half]

        for q, out in enumerate(refs[-2:]):
            out[0] = total[q, half:]

    specs = [pl.BlockSpec((2, half, cols), lambda i: (0, 0, 0))] * (count // 2)
    specs += [pl.BlockSpec((1, half, cols), lambda i: (i, 0, 0))] * 2
    shapes = [struct(2, half, cols)] * (count // 2) + [struct(count // 2, half, cols)] * 2
    return sum_call(body, own, back, behind, specs, shapes, "split_sums")


def two_parts(rows):
    high = rows.astype(BF)
    low = (rows - high.astype(F32)).astype(BF)
    return jnp.concatenate([high, low, jnp.zeros((12, rows.shape[1]), BF)])


def from_parts(rows):
    return rows[:2].astype(F32) + rows[2:4].astype(F32)


def local(tokens, gain, gate_saved, up_saved, out_grad, gate_weight, up_weight, down_weight):
    zh, x_at, zl, y, c = (lax.axis_index(a) for a in AXES)
    near = [zl * 4 + (y + k) % 4 for k in (0, 2, 3, 1)]
    far = [(1 - zl) * 4 + (y + k) % 4 for k in (0, 2, 3, 1)]
    places = [p for pair in zip(near, far) for p in pair]
    order = [((zh + q) % 2) * 4 + (x_at + r) % 4 for r in range(4) for q in range(2)]
    scalars = jnp.stack(places + [c] + order).astype(jnp.int32)

    d_z = send(out_grad, zl=1)
    d_2 = send(out_grad, y=2)
    gate4 = gate_saved.reshape(8, 2, ROWS, F)
    up4 = up_saved.reshape(8, 2, ROWS, F)
    normed_t, pack = first_call(
        scalars, tokens, gain.reshape(1, D), gate4, up4, gate_weight, up_weight, down_weight
    )
    pack = send(after(pack, d_z, d_2), c=1)
    weights = (down_weight, gate_weight, up_weight, pack)

    d_pair = jnp.stack([out_grad, after(d_z, d_2)])
    d_m = send(d_pair, y=1)
    d_p = send(d_pair, y=-1)
    d_z2 = send(d_2, zl=1)
    *factors, act_own = factor_call(scalars, after(gate4, d_pair), up4, False)
    normed_b = after(normed_t, pack, act_own)
    u_z = send(normed_b, zl=1)
    u_2 = send(normed_b, y=2)
    *others, act_oth = factor_call(scalars, pack, pack, True)
    factors += others
    dy_a, dy_b = (out_grad, d_z, d_2, d_z2), (d_m, d_p)
    gd_a, ud_a, n_own, n_z, n_2, n_z2 = delta_call(False, dy_a, factors, weights)
    u_pair = jnp.stack([normed_t, after(u_z, u_2, gd_a)])
    u_m = send(u_pair, y=1)
    u_p = send(u_pair, y=-1)
    u_z2 = send(after(u_2, gd_a), zl=1)
    down_own, down_oth = down_call(
        scalars, (act_own, act_oth), dy_a + dy_b, (gd_a, u_pair, u_2)
    )
    down_back = send(down_oth, c=1)
    gd_b, ud_b, n_ym, n_yp = delta_call(True, dy_b, factors, weights, (down_oth,))
    parts = pair_sums(down_own, down_back, (gd_b, u_z2))
    down_got = [send(parts[r], x=r) for r in (1, 2, 3)]
    a = send(n_yp, y=1)
    b = send(n_ym, y=-1)
    d = send(n_z2, zl=1)

    w_args = (
        scalars,
        (gd_a, gd_b, ud_a, ud_b),
        (normed_t, u_z, u_2, u_z2, u_m, u_p),
        (gate_weight, up_weight),
        pack,
    )
    own_0, oth_0, gain_0 = weight_call((0,), *w_args, [parts[0], d])
    own_r, oth_r, gain_r = weight_call((1, 2, 3), *w_args, [own_0])
    back_r = send(after(oth_r, a, b, *down_got), c=1)
    f = send(total_of(after(n_z, oth_r), a[1], b[1]).astype(BF), zl=1)
    *up_r, low_same, low_other = split_sums(own_r, back_r)
    up_got = [send(up_r[r - 1], x=r) for r in (1, 2, 3)]
    gain_rows = jnp.concatenate([jnp.sum(g, axis=-1) for g in (gain_0, gain_r)])
    gain_rows = jnp.roll(gain_rows.reshape(4, 2, 256), (x_at, zh), (0, 1))
    gain_rows = gain_rows.transpose(1, 0, 2).reshape(D)
    gain_rows = gain_rows.reshape(2, 1024)
    low_got = send(jnp.concatenate([low_other.reshape(384, 1024), two_parts(gain_rows)]), zh=1)
    gain_rows = gain_rows + from_parts(low_got[384:])
    low_got = low_got[:384].reshape(3, 128, 1024)
    back_0 = send(after(oth_0, low_other), c=1)
    part_0 = total_of(own_0, back_0)
    down_both = total_of(parts[0], *(after(g, low_other) for g in down_got))
    down_last = send(down_both[1].astype(BF), zh=1)
    e = send(total_of(n_2, after(d, low_other)).astype(BF), y=2)
    token_grad = last_call(tokens, out_grad, gain.reshape(1, D), n_own, a, b, e, f, ())

    up_got = [after(g, token_grad) for g in up_got]
    gain_rows = after(gain_rows, *up_got)
    gain_rows = gain_rows + send(gain_rows, c=1)
    low_sum = total_of(low_same, low_got)
    low_x = [
        send(jnp.concatenate([low_sum[r - 1].astype(BF), two_parts(gain_rows)]), x=r)
        for r in (1, 2, 3)
    ]
    gain_rows = gain_rows + total_of(*(from_parts(g[128:]) for g in low_x))
    up_sum = total_of(part_0[:, :128], *up_got)
    rest = send(jnp.concatenate([up_sum[1], part_0[1, 128:]]).astype(BF), zh=1)
    gain_rows = total_of(gain_rows, *(send(gain_rows, y=k) for k in (1, 2, 3)))
    gain_rows = after(gain_rows, rest)
    gain_rows = gain_rows + send(gain_rows, zl=1)
    gain_rows = gain_rows.reshape(D) / gain
    low_all = total_of(part_0[0, 128:], rest[128:], *(g[:128] for g in low_x))
    both_sum = jnp.concatenate([total_of(up_sum[0], rest[:128]), low_all])
    return (
        token_grad,
        gain_rows,
        both_sum[:, :F].astype(BF),
        both_sum[:, F:].astype(BF),
        (down_both[0] + down_last.astype(F32)).astype(BF),
    )


def solution(mesh):
    mesh = Mesh(mesh.devices.reshape(SIZES), AXES)
    dp, tensor = ("zh", "x"), ("zl", "y", "c")
    placed = (
        P(dp + tensor, None),
        P(),
        P(dp, tensor),
        P(dp, tensor),
        P(dp + tensor, None),
        P(None, tensor),
        P(None, tensor),
        P(tensor, None),
    )
    return jax.shard_map(
        local,
        mesh=mesh,
        in_specs=placed,
        out_specs=(
            P(dp + tensor, None),
            P(),
            P(dp, tensor),
            P(dp, tensor),
            P(tensor, dp),
        ),
        check_vma=False,
    )
```

```python
import functools

import jax
import jax.numpy as jnp
import numpy as np
from jax import lax
from jax.experimental import pallas as pl
from jax.experimental.pallas import tpu as pltpu
from jax.sharding import Mesh, PartitionSpec as P

AXES = ("zh", "x", "zl", "y", "c")
SIZES = (2, 4, 2, 4, 2)
D = 2048
ROWS = 128
F = 512
BF = jnp.bfloat16
F32 = jnp.float32
MIB = 1024 * 1024
UPPER = 112
LOWER = 256 - UPPER
ANY = pl.BlockSpec(memory_space=pl.ANY)


def send(value, **shift):
    ids = np.arange(128).reshape(SIZES)
    pairs = []
    for at in np.ndindex(*SIZES):
        to = tuple((a + shift.get(n, 0)) % s for a, n, s in zip(at, AXES, SIZES))
        pairs.append((int(ids[at]), int(ids[to])))
    return lax.ppermute(value, AXES, pairs)


def nt(a, b):
    return lax.dot_general(a, b, (((1,), (1,)), ((), ())), preferred_element_type=F32)


def nn(a, b):
    return lax.dot_general(a, b, (((1,), (0,)), ((), ())), preferred_element_type=F32)


def struct(*shape, dtype=BF):
    return jax.ShapeDtypeStruct(shape, dtype)


def params():
    return pltpu.CompilerParams(vmem_limit_bytes=38 * MIB)


def cost(mults=0):
    return pl.CostEstimate(flops=2 * mults + 1024, bytes_accessed=1024, transcendentals=0)


def after(value, *others):
    return lax.optimization_barrier((value, *others))[0]


def first_kernel(s_ref, tokens, gain, gate, up, wg, wu, wd, normed_t, pack):
    @pl.when(pl.program_id(0) == 0)
    def _():
        x = tokens[...].astype(F32)
        unit = x * lax.rsqrt(jnp.mean(x * x, axis=-1, keepdims=True) + 1e-05)
        normed_t[...] = (unit * gain[...]).astype(BF).T

    for j in range(2):
        pack[j, :128] = gate[j, 0]
        pack[j, 128:256] = up[j, 0]
        pack[j, 256:512] = wg[j * 256 : j * 256 + 256]
        pack[j, 512:768] = wu[j * 256 : j * 256 + 256]
        for k in range(4):
            at = 768 + k * 64
            pack[j, at : at + 64] = wd[j * 64 : j * 64 + 64, k * F : k * F + F]


def first_call(scalars, tokens, gain, gate4, up4, wg, wu, wd):
    half = pl.BlockSpec((2, 1, ROWS, F), lambda i, s: (i, 1 - s[8], 0, 0))
    rows = pl.BlockSpec((512, F), lambda i, s: (i, 0))
    return pl.pallas_call(
        first_kernel,
        grid_spec=pltpu.PrefetchScalarGridSpec(
            num_scalar_prefetch=1,
            grid=(4,),
            in_specs=[
                pl.BlockSpec((ROWS, D), lambda i, s: (0, 0)),
                pl.BlockSpec((1, D), lambda i, s: (0, 0)),
                half,
                half,
                rows,
                rows,
                pl.BlockSpec((128, D), lambda i, s: (i, 0)),
            ],
            out_specs=[
                pl.BlockSpec((D, ROWS), lambda i, s: (0, 0)),
                pl.BlockSpec((2, 1024, F), lambda i, s: (i, 0, 0)),
            ],
        ),
        out_shape=[struct(D, ROWS), struct(8, 1024, F)],
        compiler_params=params(),
        cost_estimate=cost(),
        name="first",
    )(scalars, tokens, gain, gate4, up4, wg, wu, wd)


def factor_kernel(s_ref, gate, up, for_gate, for_up, act_t):
    g = gate[...].astype(F32)
    u = up[...].astype(F32)
    sigma = 0.5 + 0.5 * jnp.tanh(0.5 * g)
    silu = g * sigma
    for_up[...] = silu.astype(BF)
    for_gate[...] = (u * sigma * (1.0 + g * (1.0 - sigma))).astype(BF)
    act_t[...] = (silu * u).astype(BF).T


def factor_call(scalars, gate, up, other):
    if other:
        specs = [pl.BlockSpec((None, ROWS, F), lambda i, s, k=k: (s[i], k, 0)) for k in range(2)]
    else:
        specs = [pl.BlockSpec((None, None, ROWS, F), lambda i, s: (s[i], s[8], 0, 0))] * 2
    rows = pl.BlockSpec((ROWS, F), lambda i, s: (i, 0))
    return pl.pallas_call(
        factor_kernel,
        grid_spec=pltpu.PrefetchScalarGridSpec(
            num_scalar_prefetch=1,
            grid=(8,),
            in_specs=specs,
            out_specs=[rows, rows, pl.BlockSpec((F, ROWS), lambda i, s: (0, i))],
        ),
        out_shape=[struct(8 * ROWS, F)] * 2 + [struct(F, 8 * ROWS)],
        compiler_params=params(),
        cost_estimate=cost(),
        name="factors_other" if other else "factors_own",
    )(scalars, gate, up)


def delta_body(dy, factors, weights, gd, ud, outs, held, sem):
    wd, wg, wu, pack = weights
    wd_own, wd_oth, wg_own, wg_oth, wu_own, wu_oth = held
    moves = ((wd, wd_own), (pack.at[:, 768:1024], wd_oth), (wg, wg_own))
    moves += ((pack.at[:, 256:512], wg_oth), (wu, wu_own), (pack.at[:, 512:768], wu_oth))
    copies = [pltpu.make_async_copy(a, b, sem.at[k]) for k, (a, b) in enumerate(moves)]
    for copy in copies:
        copy.start()
    rows = jnp.concatenate(dy, axis=0)

    def store(hidden, at):
        for_gate, for_up = factors[2:] if at.start else factors[:2]
        gd[:, at] = (hidden * for_gate[...].astype(F32)).astype(BF)
        ud[:, at] = (hidden * for_up[...].astype(F32)).astype(BF)

    copies[0].wait()
    store(nt(rows, wd_own[...]), slice(0, F))
    copies[1].wait()
    hidden = 0
    for k in range(4):
        block = wd_oth[:, k * 64 : k * 64 + 64, :].reshape(F, F)
        hidden = hidden + nt(rows[:, k * F : k * F + F], block)
    store(hidden, slice(F, 2 * F))
    for copy in copies[2:]:
        copy.wait()
    for n in range(4):
        at, two = slice(n * 512, n * 512 + 512), slice(2 * n, 2 * n + 2)
        out = nt(gd[:, :F], wg_own[at, :])
        out = out + nt(gd[:, F:], wg_oth[two].reshape(F, F))
        out = out + nt(ud[:, :F], wu_own[at, :])
        out = (out + nt(ud[:, F:], wu_oth[two].reshape(F, F))).astype(BF)
        for k, ref in enumerate(outs):
            ref[:, at] = out[k * ROWS : k * ROWS + ROWS]


def delta_kernel_a(*refs):
    dy = [r[...] for r in refs[:4]]
    gd, ud, *outs = refs[-13:-7]
    delta_body(dy, refs[4:8], refs[8:12], gd, ud, outs, refs[-7:-1], refs[-1])


def delta_kernel_b(*refs):
    dy = [r[k] for r in refs[:2] for k in range(2)]
    gd, ud, ym, yp = refs[-11:-7]
    outs = (ym.at[0], ym.at[1], yp.at[0], yp.at[1])
    delta_body(dy, refs[2:6], refs[6:10], gd, ud, outs, refs[-7:-1], refs[-1])


def delta_call(second, dy, factors, weights, behind=()):
    at = 1 if second else 0
    wide = pl.BlockSpec((4 * ROWS, F), lambda i: (at, 0))
    here = pl.BlockSpec((4 * ROWS, 2 * F), lambda i: (0, 0))
    if second:
        count, piece = 2, struct(2, ROWS, D)
        spec = pl.BlockSpec((2, ROWS, D), lambda i: (0, 0, 0))
    else:
        count, piece = 4, struct(ROWS, D)
        spec = pl.BlockSpec((ROWS, D), lambda i: (0, 0))
    return pl.pallas_call(
        delta_kernel_b if second else delta_kernel_a,
        grid=(1,),
        in_specs=[spec] * count + [wide] * 4 + [ANY] * 4 + [ANY] * len(behind),
        out_specs=[here, here] + [spec] * count,
        out_shape=[struct(4 * ROWS, 2 * F)] * 2 + [piece] * count,
        scratch_shapes=[pltpu.VMEM((F, D), BF), pltpu.VMEM((8, 256, F), BF)]
        + [pltpu.VMEM((D, F), BF), pltpu.VMEM((8, 256, F), BF)] * 2
        + [pltpu.SemaphoreType.DMA((6,))],
        compiler_params=params(),
        cost_estimate=cost(),
        name="deltas_b" if second else "deltas_a",
    )(*dy, *factors, *weights, *behind)


def down_kernel(s_ref, act_own, act_oth, *refs):
    out_own, out_oth = refs[-2:]
    for q in range(2):
        dy = refs[6 * q : 6 * q + 6]
        cols = [d[...] for d in dy[:4]] + [d[k] for d in dy[4:] for k in range(2)]
        cols = jnp.concatenate(cols, axis=0)
        out_own[q] = nn(act_own[...], cols).astype(BF)
        out_oth[q] = nn(act_oth[...], cols).astype(BF)


def down_call(scalars, acts, dy, behind):
    specs = [pl.BlockSpec((F, 8 * ROWS), lambda i, s: (0, 0))] * 2
    for q in range(2):
        specs += [pl.BlockSpec((ROWS, 256), lambda i, s, q=q: (0, s[9 + 2 * i + q]))] * 4
        specs += [pl.BlockSpec((2, ROWS, 256), lambda i, s, q=q: (0, 0, s[9 + 2 * i + q]))] * 2
    return pl.pallas_call(
        down_kernel,
        grid_spec=pltpu.PrefetchScalarGridSpec(
            num_scalar_prefetch=1,
            grid=(4,),
            in_specs=specs + [ANY] * len(behind),
            out_specs=[pl.BlockSpec((2, F, 256), lambda i, s: (i, 0, 0))] * 2,
        ),
        out_shape=[struct(8, F, 256)] * 2,
        compiler_params=params(),
        cost_estimate=cost(),
        name="down",
    )(scalars, *acts, *dy, *dy, *behind)


def weight_kernel(s_ref, gda, gdb, uda, udb, *refs):
    out_own, out_oth, out_gain = refs[-3:]
    for q in range(2):
        unit, (wgo, wuo, wgx, wux) = refs[10 * q : 10 * q + 6], refs[10 * q + 6 : 10 * q + 10]
        low = jnp.concatenate([u[...] for u in unit[:4]], axis=1)
        high = jnp.concatenate([u[k] for u in unit[4:] for k in range(2)], axis=1)
        total = jnp.zeros((256, 128), F32)
        for da, db, at, w_own, w_oth in (
            (gda, gdb, 0, wgo[...], wgx[0]),
            (uda, udb, F, wuo[...], wux[0]),
        ):
            for half, w, out in ((0, w_own, out_own), (F, w_oth, out_oth)):
                grad = nn(low, da[:, half : half + F]) + nn(high, db[:, half : half + F])
                out[q, :, at : at + F] = grad.astype(BF)
                prod = grad * w.astype(F32)
                for k in range(4):
                    total = total + prod[:, k * 128 : (k + 1) * 128]
        out_gain[q] = total


def weight_call(places, scalars, deltas, unit, own, pack, behind):
    count = len(places)
    step = places[1] - places[0] if count > 1 else 0

    def row(i, s, q):
        return s[9 + 2 * (places[0] + step * i) + q]

    full = pl.BlockSpec((4 * ROWS, 2 * F), lambda i, s: (0, 0))
    specs, args = [full] * 4, list(deltas)
    for q in range(2):
        at = lambda i, s, q=q: (row(i, s, q), 0)
        specs += [pl.BlockSpec((256, ROWS), at)] * 4
        specs += [pl.BlockSpec((2, 256, ROWS), lambda i, s, q=q: (0, row(i, s, q), 0))] * 2
        specs += [pl.BlockSpec((256, F), at)] * 2
        for k in (1, 2):
            specs.append(pl.BlockSpec((1, 256, F), lambda i, s, q=q, k=k: (row(i, s, q), k, 0)))
        args += [*unit, *own, pack, pack]
    specs += [ANY] * len(behind)
    args += behind
    return pl.pallas_call(
        weight_kernel,
        grid_spec=pltpu.PrefetchScalarGridSpec(
            num_scalar_prefetch=1,
            grid=(count,),
            in_specs=specs,
            out_specs=[pl.BlockSpec((2, 256, 2 * F), lambda i, s: (i, 0, 0))] * 2
            + [pl.BlockSpec((2, 256, 128), lambda i, s: (i, 0, 0))],
        ),
        out_shape=[struct(2 * count, 256, 2 * F)] * 2 + [struct(2 * count, 256, 128, dtype=F32)],
        compiler_params=params(),
        cost_estimate=cost(),
        name="weights_" + "_".join(str(r) for r in places),
    )(scalars, *args)


def last_kernel(tokens, dy, gain, own, a, b, e, f, *refs):
    x = tokens[...].astype(F32)
    inverse = lax.rsqrt(jnp.mean(x * x, axis=-1, keepdims=True) + 1e-05)
    unit = x * inverse
    normed_grad = total_of(own[...], a[0], b[0], e[...], f[...])
    scaled = gain[...] * normed_grad
    mean_term = jnp.mean(scaled * unit, axis=-1, keepdims=True)
    refs[-1][...] = (dy[...].astype(F32) + inverse * (scaled - unit * mean_term)).astype(BF)


def last_call(tokens, dy, gain, own, a, b, e, f, behind):
    rows = pl.BlockSpec((32, D), lambda i: (i, 0))
    first = pl.BlockSpec((1, 32, D), lambda i: (0, i, 0))
    return pl.pallas_call(
        last_kernel,
        grid=(4,),
        in_specs=[rows, rows, pl.BlockSpec((1, D), lambda i: (0, 0)), rows, first, first, rows, rows]
        + [ANY] * len(behind),
        out_specs=rows,
        out_shape=struct(ROWS, D),
        compiler_params=params(),
        cost_estimate=cost(),
        name="last",
    )(tokens, dy, gain, own, a, b, e, f, *behind)


def total_of(*terms):
    out = terms[0].astype(F32)
    for term in terms[1:]:
        out = out + term.astype(F32)
    return out


def sum_call(body, own, back, behind, out_specs, out_shape, name):
    block = pl.BlockSpec((2, *own.shape[1:]), lambda i: (i, 0, 0))
    return pl.pallas_call(
        body,
        grid=(own.shape[0] // 2,),
        in_specs=[block, block] + [ANY] * len(behind),
        out_specs=out_specs,
        out_shape=out_shape,
        compiler_params=params(),
        cost_estimate=cost(),
        name=name,
    )(own, back, *behind)


def pair_sums(own, back, behind=()):
    count, rows, cols = own.shape

    def body(own, back, *refs):
        total = total_of(own[...], back[...]).astype(BF)
        for r, out in enumerate(refs[len(behind) :]):

            @pl.when(pl.program_id(0) == r)
            def _():
                out[...] = total

    specs = [pl.BlockSpec((2, rows, cols), lambda i: (0, 0, 0))] * (count // 2)
    shapes = [struct(2, rows, cols)] * (count // 2)
    return sum_call(body, own, back, behind, specs, shapes, "pair_sums")


def split_sums(own, back, behind=()):
    count, rows, cols = own.shape

    def body(own, back, *refs):
        refs = refs[len(behind) :]
        total = total_of(own[...], back[...]).astype(BF)
        for r, out in enumerate(refs[:-2]):

            @pl.when(pl.program_id(0) == r)
            def _():
                out[...] = total[:, :UPPER]

        for q, out in enumerate(refs[-2:]):
            out[0] = total[q, UPPER:]

    specs = [pl.BlockSpec((2, UPPER, cols), lambda i: (0, 0, 0))] * (count // 2)
    specs += [pl.BlockSpec((1, LOWER, cols), lambda i: (i, 0, 0))] * 2
    shapes = [struct(2, UPPER, cols)] * (count // 2) + [struct(count // 2, LOWER, cols)] * 2
    return sum_call(body, own, back, behind, specs, shapes, "split_sums")


def two_parts(rows):
    high = rows.astype(BF)
    low = (rows - high.astype(F32)).astype(BF)
    return jnp.concatenate([high, low, jnp.zeros((12, rows.shape[1]), BF)])


def from_parts(rows):
    return rows[:2].astype(F32) + rows[2:4].astype(F32)


def local(tokens, gain, gate_saved, up_saved, out_grad, gate_weight, up_weight, down_weight):
    zh, x_at, zl, y, c = (lax.axis_index(a) for a in AXES)
    near = [zl * 4 + (y + k) % 4 for k in (0, 2, 3, 1)]
    far = [(1 - zl) * 4 + (y + k) % 4 for k in (0, 2, 3, 1)]
    places = [p for pair in zip(near, far) for p in pair]
    order = [((zh + q) % 2) * 4 + (x_at + r) % 4 for r in range(4) for q in range(2)]
    scalars = jnp.stack(places + [c] + order).astype(jnp.int32)

    d_z = send(out_grad, zl=1)
    d_2 = send(out_grad, y=2)
    gate4 = gate_saved.reshape(8, 2, ROWS, F)
    up4 = up_saved.reshape(8, 2, ROWS, F)
    normed_t, pack = first_call(
        scalars, tokens, gain.reshape(1, D), gate4, up4, gate_weight, up_weight, down_weight
    )
    pack = send(after(pack, d_z, d_2), c=1)
    weights = (down_weight, gate_weight, up_weight, pack)

    d_pair = jnp.stack([out_grad, after(d_z, d_2)])
    d_m = send(d_pair, y=1)
    d_p = send(d_pair, y=-1)
    d_z2 = send(d_2, zl=1)
    *factors, act_own = factor_call(scalars, after(gate4, d_pair), up4, False)
    normed_b = after(normed_t, pack, act_own)
    u_z = send(normed_b, zl=1)
    u_2 = send(normed_b, y=2)
    *others, act_oth = factor_call(scalars, pack, pack, True)
    factors += others
    dy_a, dy_b = (out_grad, d_z, d_2, d_z2), (d_m, d_p)
    gd_a, ud_a, n_own, n_z, n_2, n_z2 = delta_call(False, dy_a, factors, weights)
    u_pair = jnp.stack([normed_t, after(u_z, u_2, gd_a)])
    u_m = send(u_pair, y=1)
    u_p = send(u_pair, y=-1)
    u_z2 = send(after(u_2, gd_a), zl=1)
    down_own, down_oth = down_call(
        scalars, (act_own, act_oth), dy_a + dy_b, (gd_a, u_pair, u_2)
    )
    down_back = send(down_oth, c=1)
    gd_b, ud_b, n_ym, n_yp = delta_call(True, dy_b, factors, weights, (down_oth,))
    parts = pair_sums(down_own, down_back, (gd_b, u_z2))
    down_got = [send(parts[r], x=r) for r in (1, 2, 3)]
    a = send(n_yp, y=1)
    b = send(n_ym, y=-1)
    d = send(n_z2, zl=1)

    w_args = (
        scalars,
        (gd_a, gd_b, ud_a, ud_b),
        (normed_t, u_z, u_2, u_z2, u_m, u_p),
        (gate_weight, up_weight),
        pack,
    )
    own_0, oth_0, gain_0 = weight_call((0,), *w_args, [parts[0], d])
    own_r, oth_r, gain_r = weight_call((1, 2, 3), *w_args, [own_0])
    back_r = send(after(oth_r, a, b, *down_got), c=1)
    f = send(total_of(after(n_z, oth_r), a[1], b[1]).astype(BF), zl=1)
    gain_rows = jnp.concatenate([jnp.sum(g, axis=-1) for g in (gain_0, gain_r)])
    gain_rows = jnp.roll(gain_rows.reshape(4, 2, 256), (x_at, zh), (0, 1))
    gain_rows = gain_rows.transpose(1, 0, 2).reshape(D)
    gain_rows = gain_rows.reshape(2, 1024)
    gain_rows = total_of(
        gain_rows, send(gain_rows, c=1), send(gain_rows, zl=1), send(gain_rows, zl=1, c=1)
    )
    *up_r, low_same, low_other = split_sums(own_r, back_r, (gain_rows,))
    up_got = [send(up_r[r - 1], x=r) for r in (1, 2, 3)]
    low_got = send(jnp.concatenate([low_other.reshape(3 * LOWER, 1024), two_parts(gain_rows)]), zh=1)
    gain_rows = gain_rows + from_parts(low_got[3 * LOWER :])
    low_got = low_got[: 3 * LOWER].reshape(3, LOWER, 1024)
    back_0 = send(after(oth_0, low_other), c=1)
    part_0 = total_of(own_0, back_0)
    down_both = total_of(parts[0], *(after(g, low_other) for g in down_got))
    down_last = send(down_both[1].astype(BF), zh=1)
    e = send(total_of(n_2, after(d, low_other)).astype(BF), y=2)
    token_grad = last_call(tokens, out_grad, gain.reshape(1, D), n_own, a, b, e, f, ())

    up_got = [after(g, token_grad) for g in up_got]
    low_sum = total_of(low_same, after(low_got, *up_got))
    low_x = [
        send(jnp.concatenate([low_sum[r - 1].astype(BF), two_parts(gain_rows)]), x=r)
        for r in (1, 2, 3)
    ]
    gain_rows = gain_rows + total_of(*(from_parts(g[LOWER:]) for g in low_x))
    up_sum = total_of(part_0[:, :UPPER], *up_got)
    rest = send(jnp.concatenate([up_sum[1], part_0[1, UPPER:]]).astype(BF), zh=1)
    gain_rows = total_of(gain_rows, *(send(gain_rows, y=k) for k in (1, 2, 3)))
    gain_rows = after(gain_rows, rest)
    gain_rows = gain_rows.reshape(D) / gain
    low_all = total_of(part_0[0, UPPER:], rest[UPPER:], *(g[:LOWER] for g in low_x))
    both_sum = jnp.concatenate([total_of(up_sum[0], rest[:UPPER]), low_all])
    return (
        token_grad,
        gain_rows,
        both_sum[:, :F].astype(BF),
        both_sum[:, F:].astype(BF),
        (down_both[0] + down_last.astype(F32)).astype(BF),
    )


def solution(mesh):
    mesh = Mesh(mesh.devices.reshape(SIZES), AXES)
    dp, tensor = ("zh", "x"), ("zl", "y", "c")
    placed = (
        P(dp + tensor, None),
        P(),
        P(dp, tensor),
        P(dp, tensor),
        P(dp + tensor, None),
        P(None, tensor),
        P(None, tensor),
        P(tensor, None),
    )
    return jax.shard_map(
        local,
        mesh=mesh,
        in_specs=placed,
        out_specs=(
            P(dp + tensor, None),
            P(),
            P(dp, tensor),
            P(dp, tensor),
            P(tensor, dp),
        ),
        check_vma=False,
    )
```
